128 devices in a mesh: gx: 8 (over y, z_lo), gy: 4 (over x), ft: 4 (over z_hi, core).
Axes of the slice: x: 4, y: 4, z: 4 (z_hi: 2, z_lo: 2; z = z_hi * 2 + z_lo), core: 2. Of those that a mesh axis runs over, the one named last changes fastest.
Arguments:
- wind_field: bfloat16 [16, 16, 2048, 512], P('ft', None, 'gx', 'gy'), may hold values from -6 to 6
- terrain: int32 [2048, 512], P('gx', 'gy'), may hold values from 0 to 8
- start_basis: float32 [2048, 256], P('gx'), may hold values from -6 to 6
Outputs:
- advanced: bfloat16 [16, 16, 2048, 512], P('ft', None, 'gx', 'gy')
- basis: float32 [2048, 256], P('gx')
- core: bfloat16 [256, 16, 16, 512], P('gx', 'ft', None, 'gy')
The draws below stay inside these ranges and needn't reach their ends.
All inputs are finite; a program needn't handle non-finite values.
Results may differ from the reference program's by a relative error of at most 0.0065.
Values may be sent and summed in bfloat16 or wider, within the bound.
A program may use at most 128 MiB of HBM per device.

```python
import jax
import jax.numpy as jnp
from jax import lax

NF = 16
NZ = 16
R = 256
ITERS = 4
NX = 2048
NY = 512


def plant(entries, stream_key, smallest, top_value):
    extent = entries.shape
    spot = [jax.random.randint(jax.random.fold_in(stream_key, axis), (), 0, extent[axis]) for axis in range(len(extent))]
    entries = entries.at[tuple(spot)].set(smallest)
    longest = extent.index(max(extent))
    spot[longest] = (spot[longest] + 1) % extent[longest]
    return entries.at[tuple(spot)].set(top_value)


def shard_levels(key, extent, pieces, smallest, largest):
    loudness = 1.0
    for position, blocks in pieces:
        steps = jax.random.uniform(jax.random.fold_in(jax.random.fold_in(key, 6), position), (blocks,), jnp.float32, smallest / len(pieces), largest / len(pieces))
        loudness = loudness * jnp.repeat(jnp.exp(steps), extent[position] // blocks).reshape((-1,) + (1,) * (len(extent) - 1 - position))
    return loudness


def scatter_about(rng, dims, scale, reach, shards=(), kind=jnp.bfloat16):
    drawn = jax.random.normal(rng, dims, jnp.float32) * scale
    if len(shards) > 0:
        drawn = shard_levels(rng, dims, shards, -0.22, 0.18) * drawn
    return jnp.clip(drawn, min=-reach, max=reach).astype(kind)


def setup_inputs(seed: int = 0) -> dict:
    splits = jax.random.split(jax.random.key(seed), 4)
    wind_field = scatter_about(splits[0], (NF, NZ, NX, NY), 1.0, 6.0, ((0, 4), (2, 8), (3, 4)))
    terrain = plant(jax.random.randint(splits[1], (NX, NY), 0, NZ // 2 + 1), jax.random.fold_in(splits[1], 1), 0, (NZ // 2 + 1) - 1).astype(jnp.int32)
    start_basis = scatter_about(splits[2], (NX, R), 1.0, 6.0, ((0, 8),), jnp.float32)
    return {"wind_field": wind_field, "terrain": terrain, "start_basis": start_basis}


diffusion_number = 0.15

def reference(wind_field, terrain, start_basis):
    values = wind_field.astype(jnp.float32)
    vertical = jnp.pad(values, ((0, 0), (1, 1), (0, 0), (0, 0)))
    neighbours = vertical[:, 2:] + vertical[:, :-2]
    neighbours = neighbours + jnp.roll(values, 1, 2) + jnp.roll(values, -1, 2)
    neighbours = neighbours + jnp.roll(values, 1, 3) + jnp.roll(values, -1, 3)
    stepped = values + diffusion_number * (neighbours - 6.0 * values)
    level_index = jnp.arange(NZ).astype(jnp.int32)[:, None, None]
    keep = level_index >= terrain.astype(jnp.int32)[None]
    advanced = jnp.where(keep[None], stepped, jnp.float32(0.0)).astype(jnp.bfloat16)
    matrix = jnp.transpose(advanced, (2, 0, 1, 3)).reshape(NX, NF * NZ * NY)
    gram_rows = jnp.dot(matrix.astype(jnp.float32), matrix.T.astype(jnp.float32), preferred_element_type=jnp.float32)
    basis = start_basis
    for iteration in range(ITERS):
        image = jnp.dot(gram_rows.astype(jnp.float32), basis.astype(jnp.float32), precision=lax.Precision.HIGHEST, preferred_element_type=jnp.float32)
        cross = jnp.dot(image.T.astype(jnp.float32), image.astype(jnp.float32), precision=lax.Precision.HIGHEST, preferred_element_type=jnp.float32)
        factor = jnp.linalg.cholesky(cross)
        basis = lax.linalg.triangular_solve(factor, image, left_side=False, lower=True, transpose_a=True)
    rounded = basis.astype(jnp.bfloat16)
    core = jnp.dot(rounded.T.astype(jnp.float32), matrix.astype(jnp.float32), preferred_element_type=jnp.float32).astype(jnp.bfloat16)
    return (advanced, basis, core.reshape(R, NF, NZ, NY))
```

```python
import functools

import jax
import jax.numpy as jnp
from jax import lax
from jax.experimental import pallas as pl
from jax.experimental.pallas import tpu as pltpu
from jax.sharding import PartitionSpec as P

ITERS = 4
MESH = pl.DeviceIdType.MESH
VMEM = pltpu.VMEM
F32 = jnp.float32
BF16 = jnp.bfloat16
GX = 8
BLOCK = 256
PAIRS = 36
LIMIT = 56 * 1024 * 1024

diffusion_number = 0.15


def place():
    return lax.axis_index("gx"), lax.axis_index("gy"), lax.axis_index("ft")


def greet(devices):
    barrier = pltpu.get_barrier_semaphore()
    for device in devices:
        pl.semaphore_signal(barrier, inc=1, device_id=device, device_id_type=MESH)
    pl.semaphore_wait(barrier, len(devices))


def remote(src, dst, send, recv, device):
    return pltpu.make_async_remote_copy(
        src_ref=src, dst_ref=dst, send_sem=send, recv_sem=recv, device_id=device, device_id_type=MESH
    )


def step_kernel(
    wind, terrain, advanced, rows,
    edge_out, edge_in, line_out, line_in, merged, near_x, near_y,
    halo_send, halo_recv, send_sem, recv_sem, local_sem,
):
    gx, gy, ft = place()
    peers = [(lax.rem(gx + i, GX), gy, ft) for i in range(1, GX)]
    after, before = (gx, lax.rem(gy + 1, 4), ft), (gx, lax.rem(gy + 3, 4), ft)
    greet(peers + [after, before])
    lane = lax.broadcasted_iota(jnp.int32, (BLOCK, 128), 1)
    line = lax.broadcasted_iota(jnp.int32, (BLOCK, 128), 0)

    def collect(k, packed):
        tile = wind[k // 16, k % 16].astype(F32)
        line_out[0, pl.ds(k, 1), :] = tile[0:1]
        line_out[1, pl.ds(k, 1), :] = tile[BLOCK - 1 : BLOCK]
        return jnp.where(lane // 2 == k, pltpu.roll(tile, 2 * k + 1, 1), packed)

    packed = lax.fori_loop(0, 64, collect, jnp.zeros((BLOCK, 128), F32))
    edge_out[...] = packed.astype(BF16)
    halos = [
        remote(line_out.at[1], line_in.at[0], halo_send.at[0], halo_recv.at[0], peers[0]),
        remote(line_out.at[0], line_in.at[1], halo_send.at[1], halo_recv.at[1], peers[6]),
        remote(edge_out, edge_in.at[0], halo_send.at[2], halo_recv.at[2], after),
        remote(edge_out, edge_in.at[1], halo_send.at[3], halo_recv.at[3], before),
    ]
    for copy in halos:
        copy.start()
    a = lax.broadcasted_iota(jnp.int32, (BLOCK, BLOCK), 0)
    b = lax.broadcasted_iota(jnp.int32, (BLOCK, BLOCK), 1)
    near_x[...] = jnp.where(jnp.abs(a - b) == 1, 1.0, 0.0).astype(BF16)
    near_y[...] = near_x[0:128, 0:128]
    for copy in halos:
        copy.wait()
    from_before = pltpu.roll(edge_in[0].astype(F32), 1, 1)
    from_after = pltpu.roll(edge_in[1].astype(F32), 127, 1)
    merged[...] = jnp.where(lane % 2 == 0, from_after, from_before)

    def chunk(c):
        field, first = c // 2, (c % 2) * 8

        def level(i, _):
            z = first + i
            k = field * 16 + z
            tile = wind[field, z]
            center = tile.astype(F32)
            above = wind[field, lax.rem(z + 1, 16)].astype(F32)
            below = wind[field, lax.rem(z + 15, 16)].astype(F32)
            around = jnp.where(z < 15, above, 0.0) + jnp.where(z > 0, below, 0.0)
            around += jnp.dot(near_x[...], tile, preferred_element_type=F32)
            around += jnp.dot(tile, near_y[...], preferred_element_type=F32)
            side = pltpu.roll(merged[...], 127 - 2 * k, 1)
            around += jnp.where((lane == 0) | (lane == 127), side, 0.0)
            around += jnp.where(line == 0, line_in[0, pl.ds(k, 1), :], 0.0)
            around += jnp.where(line == BLOCK - 1, line_in[1, pl.ds(k, 1), :], 0.0)
            stepped = center + diffusion_number * (around - 6.0 * center)
            advanced[field, z] = jnp.where(z >= terrain[...], stepped, 0.0).astype(BF16)
            return 0

        lax.fori_loop(0, 8, level, 0)
        return advanced.at[field, pl.ds(first, 8)]

    def to_peer(i):
        c = lax.rem(gx + i, GX)
        part = advanced.at[c // 2, pl.ds((c % 2) * 8, 8)]
        return remote(part, rows.at[gx], send_sem.at[i - 1], recv_sem.at[i - 1], (c, gy, ft))

    def send_one(i, _):
        chunk(lax.rem(gx + i, GX))
        to_peer(i).start()
        return 0

    lax.fori_loop(1, GX, send_one, 0)
    own = pltpu.make_async_copy(chunk(gx), rows.at[gx], local_sem)
    own.start()

    def finish(i, _):
        copy = to_peer(i)
        copy.wait_send()
        source = lax.rem(gx + GX - i, GX)
        remote(rows.at[source], rows.at[source], send_sem.at[i - 1], recv_sem.at[i - 1], (source, gy, ft)).wait_recv()
        return 0

    lax.fori_loop(1, GX, finish, 0)
    own.wait()


def step(wind_field, terrain):
    return pl.pallas_call(
        step_kernel,
        out_shape=(
            jax.ShapeDtypeStruct((4, 16, BLOCK, 128), BF16),
            jax.ShapeDtypeStruct((GX, 8, BLOCK, 128), BF16),
        ),
        in_specs=[pl.BlockSpec(memory_space=VMEM)] * 2,
        out_specs=(pl.BlockSpec(memory_space=VMEM),) * 2,
        scratch_shapes=[
            VMEM((BLOCK, 128), BF16),
            VMEM((2, BLOCK, 128), BF16),
            VMEM((2, 64, 128), F32),
            VMEM((2, 64, 128), F32),
            VMEM((BLOCK, 128), F32),
            VMEM((BLOCK, BLOCK), BF16),
            VMEM((128, 128), BF16),
            pltpu.SemaphoreType.DMA((4,)),
            pltpu.SemaphoreType.DMA((4,)),
            pltpu.SemaphoreType.DMA((7,)),
            pltpu.SemaphoreType.DMA((7,)),
            pltpu.SemaphoreType.DMA,
        ],
        compiler_params=pltpu.CompilerParams(collective_id=0, has_side_effects=True, vmem_limit_bytes=LIMIT),
        name="step",
    )(wind_field, terrain)


HALF = 18 * BLOCK
PART = HALF // 3


def gram_kernel(
    rows, gram, partial, half_in, in_1, in_2, in_3,
    pair_send, pair_recv, send_1, recv_1, send_2, recv_2, send_3, recv_3,
    back_3, home_3, back_2, home_2, back_1, home_1, last_send, last_recv,
):
    gx, gy, ft = place()
    core = ft % 2
    coords = (gy, gx // 2, (ft // 2) * 2 + gx % 2)

    def at(axis, t):
        if axis == 0:
            return (gx, t, ft)
        if axis == 1:
            return (t * 2 + gx % 2, gy, ft)
        return ((gx // 2) * 2 + t % 2, gy, (t // 2) * 2 + ft % 2)

    def peer(axis, o):
        t = lax.rem(coords[axis] + o, 4)
        return t, at(axis, t)

    sibling = (gx, gy, (ft // 2) * 2 + 1 - core)
    greet([sibling] + [peer(axis, o)[1] for axis in range(3) for o in range(1, 4)])

    def block(s):
        j = s % 8
        i = (j + s // 8) % 8
        left = jnp.concatenate([rows[j, z] for z in range(8)], axis=1)
        right = jnp.concatenate([rows[i, z] for z in range(8)], axis=1)
        partial[pl.ds(pl.multiple_of(s * BLOCK, BLOCK), BLOCK), :] = lax.dot_general(
            left, right, (((1,), (1,)), ((), ())), preferred_element_type=F32
        )

    def blocks(first):
        lax.fori_loop(0, 18, lambda k, _: (block(first + k), 0)[1], 0)

    mine = pl.multiple_of(core * HALF, HALF)
    other = pl.multiple_of((1 - core) * HALF, HALF)
    blocks((1 - core) * 18)
    swap = remote(partial.at[pl.ds(other, HALF)], half_in, pair_send, pair_recv, sibling)
    swap.start()
    blocks(core * 18)
    swap.wait()

    def add(first, count, sources, tile):
        def body(k, _):
            here = pl.ds(pl.multiple_of(first + k * tile, 8), tile)
            there = pl.ds(pl.multiple_of(k * tile, 8), tile)
            total = partial[here, :]
            for source in sources:
                total = total + source[there, :]
            partial[here, :] = total
            return 0

        lax.fori_loop(0, count // tile, body, 0)

    add(mine, HALF, [half_in], 128)
    starts = [[mine + p * PART] for p in range(3)]
    sizes = [PART // 4, PART // 16, PART // 64]
    for depth, (inbox, send, recv) in enumerate(((in_1, send_1, recv_1), (in_2, send_2, recv_2), (in_3, send_3, recv_3))):
        size = sizes[depth]
        copies = []
        for p in range(3):
            axis = (p + depth) % 3
            for o in range(1, 4):
                t, device = peer(axis, o)
                src = pl.ds(pl.multiple_of(starts[p][depth] + t * size, 8), size)
                n = p * 3 + o - 1
                copies.append(remote(partial.at[src], inbox.at[n], send.at[n], recv.at[n], device))
        for copy in copies:
            copy.start()
        for copy in copies:
            copy.wait()
        for p in range(3):
            first = starts[p][depth] + coords[(p + depth) % 3] * size
            starts[p].append(first)
            add(first, size, [inbox.at[p * 3 + o] for o in range(3)], min(size, 96))

    for p in range(3):
        here = pl.ds(pl.multiple_of(starts[p][3], 8), sizes[2])
        gram[here, :] = partial[here, :]
    lasts = []

    def pass_on(p, first, n):
        here = gram.at[pl.ds(pl.multiple_of(first, 8), sizes[0])]
        copy = remote(here, here, last_send.at[n], last_recv.at[n], sibling)
        copy.start()
        lasts.append(copy)

    for depth, send, recv in ((2, back_3, home_3), (1, back_2, home_2), (0, back_1, home_1)):
        size = sizes[depth]
        copies = []
        for p in range(3):
            here = gram.at[pl.ds(pl.multiple_of(starts[p][depth + 1], 8), size)]
            for o in range(1, 4):
                _, device = peer((p + depth) % 3, o)
                n = p * 3 + o - 1
                copies.append(remote(here, here, send.at[n], recv.at[n], device))
        for copy in copies:
            copy.start()
        if depth == 0:
            for p in range(3):
                pass_on(p, starts[p][1], p * 4)
        arrivals = []
        for p in range(3):
            axis = (p + depth) % 3
            for o in range(1, 4):
                n = p * 3 + o - 1
                t, device = peer(axis, 4 - o)
                first = starts[p][depth] + t * size
                there = gram.at[pl.ds(pl.multiple_of(first, 8), size)]
                remote(there, there, send.at[n], recv.at[n], device).wait_recv()
                if depth == 0:
                    pass_on(p, first, p * 4 + o)
        for copy in copies:
            copy.wait_send()
    for p in range(3):
        for o in range(4):
            n = p * 4 + o
            t = lax.rem(coords[p] + 4 - o, 4)
            there = gram.at[pl.ds(pl.multiple_of(other + p * PART + t * sizes[0], 8), sizes[0])]
            remote(there, there, last_send.at[n], last_recv.at[n], sibling).wait_recv()
    for copy in lasts:
        copy.wait_send()


def gram_blocks(rows):
    dma = pltpu.SemaphoreType.DMA
    return pl.pallas_call(
        gram_kernel,
        out_shape=jax.ShapeDtypeStruct((PAIRS * BLOCK, BLOCK), F32),
        in_specs=[pl.BlockSpec(memory_space=VMEM)],
        out_specs=pl.BlockSpec(memory_space=VMEM),
        scratch_shapes=[
            VMEM((PAIRS * BLOCK, BLOCK), F32),
            VMEM((HALF, BLOCK), F32),
            VMEM((9, PART // 4, BLOCK), F32),
            VMEM((9, PART // 16, BLOCK), F32),
            VMEM((9, PART // 64, BLOCK), F32),
            dma, dma,
        ]
        + [dma((9,))] * 12
        + [dma((12,))] * 2,
        compiler_params=pltpu.CompilerParams(collective_id=1, has_side_effects=True, vmem_limit_bytes=LIMIT),
        name="gram",
    )(rows)


def core_kernel(basis_t, rows, core, stage, outbox, inbox, send_sem, recv_sem):
    gx, gy, ft = place()
    peers = [(lax.rem(gx + i, GX), gy, ft) for i in range(1, GX)]
    greet(peers)
    for z in range(0, 8, 2):
        total = jnp.zeros((BLOCK, BLOCK), F32)
        for j in range(GX):
            pair = jnp.concatenate([rows[j, z], rows[j, z + 1]], axis=1)
            total += jnp.dot(basis_t[:, j * BLOCK : (j + 1) * BLOCK], pair, preferred_element_type=F32)
        stage[:, z, :] = total[:, :128]
        stage[:, z + 1, :] = total[:, 128:]
    for r in range(GX):
        outbox[r] = stage[r * 32 : (r + 1) * 32].reshape(BLOCK, 128).astype(BF16)
    copies = []
    for i in range(1, GX):
        device = peers[i - 1]
        copies.append(remote(outbox.at[device[0]], inbox.at[gx], send_sem.at[i - 1], recv_sem.at[i - 1], device))
    for copy in copies:
        copy.start()
    inbox[gx] = outbox[gx]
    for i in range(1, GX):
        there = inbox.at[lax.rem(gx + GX - i, GX)]
        remote(there, there, send_sem.at[i - 1], recv_sem.at[i - 1], peers[GX - 1 - i]).wait_recv()
    for f in range(4):
        low = inbox[2 * f].astype(F32).reshape(32, 8, 128)
        high = inbox[2 * f + 1].astype(F32).reshape(32, 8, 128)
        core[:, f] = jnp.concatenate([low, high], axis=1).astype(BF16)
    for copy in copies:
        copy.wait_send()


def core_of(basis_t, rows):
    return pl.pallas_call(
        core_kernel,
        out_shape=jax.ShapeDtypeStruct((32, 4, 16, 128), BF16),
        in_specs=[pl.BlockSpec(memory_space=VMEM)] * 2,
        out_specs=pl.BlockSpec(memory_space=VMEM),
        scratch_shapes=[
            VMEM((BLOCK, 8, 128), F32),
            VMEM((GX, BLOCK, 128), BF16),
            VMEM((GX, BLOCK, 128), BF16),
            pltpu.SemaphoreType.DMA((7,)),
            pltpu.SemaphoreType.DMA((7,)),
        ],
        compiler_params=pltpu.CompilerParams(collective_id=2, has_side_effects=True, vmem_limit_bytes=LIMIT),
        name="core",
    )(basis_t, rows)


def whole(blocks):
    blocks = blocks.reshape(PAIRS, BLOCK, BLOCK)

    def entry(i, k):
        d = (k - i) % 8
        if d < 4:
            return blocks[d * 8 + i]
        if d > 4:
            return blocks[(8 - d) * 8 + k].T
        return blocks[32 + i] if i < 4 else blocks[32 + k].T

    return jnp.concatenate([jnp.concatenate([entry(i, k) for k in range(GX)], axis=1) for i in range(GX)], axis=0)


def per_device(wind_field, terrain, start_basis):
    basis = lax.all_gather(start_basis, "gx", axis=0, tiled=True)
    advanced, rows = step(wind_field, terrain)
    gram = whole(gram_blocks(rows))
    for iteration in range(ITERS):
        image = jnp.dot(gram, basis, precision=lax.Precision.HIGHEST, preferred_element_type=F32)
        cross = jnp.dot(image.T, image, precision=lax.Precision.HIGHEST, preferred_element_type=F32)
        factor = jnp.linalg.cholesky(cross)
        basis = lax.linalg.triangular_solve(factor, image, left_side=False, lower=True, transpose_a=True)
    basis_rows = lax.dynamic_slice_in_dim(basis, lax.axis_index("gx") * BLOCK, BLOCK, 0)
    core = core_of(basis.astype(BF16).T, rows)
    return (advanced, basis_rows, core)


def solution(mesh):
    placed = (P("ft", None, "gx", "gy"), P("gx", "gy"), P("gx", None))
    return jax.shard_map(
        per_device,
        mesh=mesh,
        in_specs=placed,
        out_specs=(P("ft", None, "gx", "gy"), P("gx", None), P("gx", "ft", None, "gy")),
        check_vma=False,
    )
```

```python
import functools

import jax
import jax.numpy as jnp
from jax import lax
from jax.experimental import pallas as pl
from jax.experimental.pallas import tpu as pltpu
from jax.sharding import PartitionSpec as P

ITERS = 4
MESH = pl.DeviceIdType.MESH
VMEM = pltpu.VMEM
F32 = jnp.float32
BF16 = jnp.bfloat16
GX = 8
BLOCK = 256
PAIRS = 36
LIMIT = 56 * 1024 * 1024

diffusion_number = 0.15


def place():
    return lax.axis_index("gx"), lax.axis_index("gy"), lax.axis_index("ft")


def greet(devices):
    barrier = pltpu.get_barrier_semaphore()
    for device in devices:
        pl.semaphore_signal(barrier, inc=1, device_id=device, device_id_type=MESH)
    pl.semaphore_wait(barrier, len(devices))


def remote(src, dst, send, recv, device):
    return pltpu.make_async_remote_copy(
        src_ref=src, dst_ref=dst, send_sem=send, recv_sem=recv, device_id=device, device_id_type=MESH
    )


def step_kernel(
    wind, terrain, advanced, rows,
    edge_out, edge_in, line_out, line_in, merged, near_x, near_y,
    halo_send, halo_recv, send_sem, recv_sem, local_sem,
):
    gx, gy, ft = place()
    peers = [(lax.rem(gx + i, GX), gy, ft) for i in range(1, GX)]
    after, before = (gx, lax.rem(gy + 1, 4), ft), (gx, lax.rem(gy + 3, 4), ft)
    greet(peers + [after, before])
    lane = lax.broadcasted_iota(jnp.int32, (BLOCK, 128), 1)
    line = lax.broadcasted_iota(jnp.int32, (BLOCK, 128), 0)

    def collect(k, packed):
        tile = wind[k // 16, k % 16].astype(F32)
        line_out[0, pl.ds(k, 1), :] = tile[0:1]
        line_out[1, pl.ds(k, 1), :] = tile[BLOCK - 1 : BLOCK]
        return jnp.where(lane // 2 == k, pltpu.roll(tile, 2 * k + 1, 1), packed)

    packed = lax.fori_loop(0, 64, collect, jnp.zeros((BLOCK, 128), F32))
    edge_out[...] = packed.astype(BF16)
    halos = [
        remote(line_out.at[1], line_in.at[0], halo_send.at[0], halo_recv.at[0], peers[0]),
        remote(line_out.at[0], line_in.at[1], halo_send.at[1], halo_recv.at[1], peers[6]),
        remote(edge_out, edge_in.at[0], halo_send.at[2], halo_recv.at[2], after),
        remote(edge_out, edge_in.at[1], halo_send.at[3], halo_recv.at[3], before),
    ]
    for copy in halos:
        copy.start()
    a = lax.broadcasted_iota(jnp.int32, (BLOCK, BLOCK), 0)
    b = lax.broadcasted_iota(jnp.int32, (BLOCK, BLOCK), 1)
    near_x[...] = jnp.where(jnp.abs(a - b) == 1, 1.0, 0.0).astype(BF16)
    near_y[...] = near_x[0:128, 0:128]
    for copy in halos:
        copy.wait()
    from_before = pltpu.roll(edge_in[0].astype(F32), 1, 1)
    from_after = pltpu.roll(edge_in[1].astype(F32), 127, 1)
    merged[...] = jnp.where(lane % 2 == 0, from_after, from_before)

    def chunk(c):
        field, first = c // 2, (c % 2) * 8

        def level(i, _):
            z = first + i
            k = field * 16 + z
            tile = wind[field, z]
            center = tile.astype(F32)
            above = wind[field, lax.rem(z + 1, 16)].astype(F32)
            below = wind[field, lax.rem(z + 15, 16)].astype(F32)
            around = jnp.where(z < 15, above, 0.0) + jnp.where(z > 0, below, 0.0)
            around += jnp.dot(near_x[...], tile, preferred_element_type=F32)
            around += jnp.dot(tile, near_y[...], preferred_element_type=F32)
            side = pltpu.roll(merged[...], 127 - 2 * k, 1)
            around += jnp.where((lane == 0) | (lane == 127), side, 0.0)
            around += jnp.where(line == 0, line_in[0, pl.ds(k, 1), :], 0.0)
            around += jnp.where(line == BLOCK - 1, line_in[1, pl.ds(k, 1), :], 0.0)
            stepped = center + diffusion_number * (around - 6.0 * center)
            advanced[field, z] = jnp.where(z >= terrain[...], stepped, 0.0).astype(BF16)
            return 0

        lax.fori_loop(0, 8, level, 0)
        return advanced.at[field, pl.ds(first, 8)]

    def to_peer(i):
        c = lax.rem(gx + i, GX)
        part = advanced.at[c // 2, pl.ds((c % 2) * 8, 8)]
        return remote(part, rows.at[gx], send_sem.at[i - 1], recv_sem.at[i - 1], (c, gy, ft))

    def send_one(i, _):
        chunk(lax.rem(gx + i, GX))
        to_peer(i).start()
        return 0

    lax.fori_loop(1, GX, send_one, 0)
    own = pltpu.make_async_copy(chunk(gx), rows.at[gx], local_sem)
    own.start()

    def finish(i, _):
        copy = to_peer(i)
        copy.wait_send()
        source = lax.rem(gx + GX - i, GX)
        remote(rows.at[source], rows.at[source], send_sem.at[i - 1], recv_sem.at[i - 1], (source, gy, ft)).wait_recv()
        return 0

    lax.fori_loop(1, GX, finish, 0)
    own.wait()


def step(wind_field, terrain):
    return pl.pallas_call(
        step_kernel,
        out_shape=(
            jax.ShapeDtypeStruct((4, 16, BLOCK, 128), BF16),
            jax.ShapeDtypeStruct((GX, 8, BLOCK, 128), BF16),
        ),
        in_specs=[pl.BlockSpec(memory_space=VMEM)] * 2,
        out_specs=(pl.BlockSpec(memory_space=VMEM),) * 2,
        scratch_shapes=[
            VMEM((BLOCK, 128), BF16),
            VMEM((2, BLOCK, 128), BF16),
            VMEM((2, 64, 128), F32),
            VMEM((2, 64, 128), F32),
            VMEM((BLOCK, 128), F32),
            VMEM((BLOCK, BLOCK), BF16),
            VMEM((128, 128), BF16),
            pltpu.SemaphoreType.DMA((4,)),
            pltpu.SemaphoreType.DMA((4,)),
            pltpu.SemaphoreType.DMA((7,)),
            pltpu.SemaphoreType.DMA((7,)),
            pltpu.SemaphoreType.DMA,
        ],
        compiler_params=pltpu.CompilerParams(collective_id=0, has_side_effects=True, vmem_limit_bytes=LIMIT),
        name="step",
    )(wind_field, terrain)


HALF = 18 * BLOCK
PART = HALF // 3


def gram_kernel(
    rows, gram, partial, half_in, in_1, in_2, in_3,
    pair_send, pair_recv, send_1, recv_1, send_2, recv_2, send_3, recv_3,
    back_3, home_3, back_2, home_2, back_1, home_1, last_send, last_recv,
):
    gx, gy, ft = place()
    core = ft % 2
    coords = (gy, gx // 2, (ft // 2) * 2 + gx % 2)

    def at(axis, t):
        if axis == 0:
            return (gx, t, ft)
        if axis == 1:
            return (t * 2 + gx % 2, gy, ft)
        return ((gx // 2) * 2 + t % 2, gy, (t // 2) * 2 + ft % 2)

    def peer(axis, o):
        t = lax.rem(coords[axis] + o, 4)
        return t, at(axis, t)

    sibling = (gx, gy, (ft // 2) * 2 + 1 - core)
    greet([sibling] + [peer(axis, o)[1] for axis in range(3) for o in range(1, 4)])

    def block(s):
        j = s % 8
        i = (j + s // 8) % 8
        left = jnp.concatenate([rows[j, z] for z in range(8)], axis=1)
        right = jnp.concatenate([rows[i, z] for z in range(8)], axis=1)
        partial[pl.ds(pl.multiple_of(s * BLOCK, BLOCK), BLOCK), :] = lax.dot_general(
            left, right, (((1,), (1,)), ((), ())), preferred_element_type=F32
        )

    def blocks(first):
        lax.fori_loop(0, 18, lambda k, _: (block(first + k), 0)[1], 0)

    mine = pl.multiple_of(core * HALF, HALF)
    other = pl.multiple_of((1 - core) * HALF, HALF)
    blocks((1 - core) * 18)
    swap = remote(partial.at[pl.ds(other, HALF)], half_in, pair_send, pair_recv, sibling)
    swap.start()
    blocks(core * 18)
    swap.wait()

    def add(first, count, sources, tile):
        def body(k, _):
            here = pl.ds(pl.multiple_of(first + k * tile, 8), tile)
            there = pl.ds(pl.multiple_of(k * tile, 8), tile)
            total = partial[here, :]
            for source in sources:
                total = total + source[there, :]
            partial[here, :] = total
            return 0

        lax.fori_loop(0, count // tile, body, 0)

    add(mine, HALF, [half_in], 128)
    starts = [[mine + p * PART] for p in range(3)]
    sizes = [PART // 4, PART // 16, PART // 64]
    for depth, (inbox, send, recv) in enumerate(((in_1, send_1, recv_1), (in_2, send_2, recv_2), (in_3, send_3, recv_3))):
        size = sizes[depth]
        copies = []
        for p in range(3):
            axis = (p + depth) % 3
            for o in range(1, 4):
                t, device = peer(axis, o)
                src = pl.ds(pl.multiple_of(starts[p][depth] + t * size, 8), size)
                n = p * 3 + o - 1
                copies.append(remote(partial.at[src], inbox.at[n], send.at[n], recv.at[n], device))
        for copy in copies:
            copy.start()
        for copy in copies:
            copy.wait()
        for p in range(3):
            first = starts[p][depth] + coords[(p + depth) % 3] * size
            starts[p].append(first)
            add(first, size, [inbox.at[p * 3 + o] for o in range(3)], min(size, 96))

    for p in range(3):
        here = pl.ds(pl.multiple_of(starts[p][3], 8), sizes[2])
        gram[here, :] = partial[here, :]
    lasts = []

    def pass_on(p, first, n):
        here = gram.at[pl.ds(pl.multiple_of(first, 8), sizes[0])]
        copy = remote(here, here, last_send.at[n], last_recv.at[n], sibling)
        copy.start()
        lasts.append(copy)

    for depth, send, recv in ((2, back_3, home_3), (1, back_2, home_2), (0, back_1, home_1)):
        size = sizes[depth]
        copies = []
        for p in range(3):
            here = gram.at[pl.ds(pl.multiple_of(starts[p][depth + 1], 8), size)]
            for o in range(1, 4):
                _, device = peer((p + depth) % 3, o)
                n = p * 3 + o - 1
                copies.append(remote(here, here, send.at[n], recv.at[n], device))
        for copy in copies:
            copy.start()
        if depth == 0:
            for p in range(3):
                pass_on(p, starts[p][1], p * 4)
        arrivals = []
        for p in range(3):
            axis = (p + depth) % 3
            for o in range(1, 4):
                n = p * 3 + o - 1
                t, device = peer(axis, 4 - o)
                first = starts[p][depth] + t * size
                there = gram.at[pl.ds(pl.multiple_of(first, 8), size)]
                remote(there, there, send.at[n], recv.at[n], device).wait_recv()
                if depth == 0:
                    pass_on(p, first, p * 4 + o)
        for copy in copies:
            copy.wait_send()
    for p in range(3):
        for o in range(4):
            n = p * 4 + o
            t = lax.rem(coords[p] + 4 - o, 4)
            there = gram.at[pl.ds(pl.multiple_of(other + p * PART + t * sizes[0], 8), sizes[0])]
            remote(there, there, last_send.at[n], last_recv.at[n], sibling).wait_recv()
    for copy in lasts:
        copy.wait_send()


def gram_blocks(rows):
    dma = pltpu.SemaphoreType.DMA
    return pl.pallas_call(
        gram_kernel,
        out_shape=jax.ShapeDtypeStruct((PAIRS * BLOCK, BLOCK), F32),
        in_specs=[pl.BlockSpec(memory_space=VMEM)],
        out_specs=pl.BlockSpec(memory_space=VMEM),
        scratch_shapes=[
            VMEM((PAIRS * BLOCK, BLOCK), F32),
            VMEM((HALF, BLOCK), F32),
            VMEM((9, PART // 4, BLOCK), F32),
            VMEM((9, PART // 16, BLOCK), F32),
            VMEM((9, PART // 64, BLOCK), F32),
            dma, dma,
        ]
        + [dma((9,))] * 12
        + [dma((12,))] * 2,
        compiler_params=pltpu.CompilerParams(collective_id=1, has_side_effects=True, vmem_limit_bytes=LIMIT),
        name="gram",
    )(rows)


def core_kernel(basis_t, rows, core, stage, outbox, inbox, send_sem, recv_sem):
    gx, gy, ft = place()
    peers = [(lax.rem(gx + i, GX), gy, ft) for i in range(1, GX)]
    greet(peers)
    for z in range(0, 8, 2):
        total = jnp.zeros((BLOCK, BLOCK), F32)
        for j in range(GX):
            pair = jnp.concatenate([rows[j, z], rows[j, z + 1]], axis=1)
            total += jnp.dot(basis_t[:, j * BLOCK : (j + 1) * BLOCK], pair, preferred_element_type=F32)
        stage[:, z, :] = total[:, :128]
        stage[:, z + 1, :] = total[:, 128:]
    for r in range(GX):
        outbox[r] = stage[r * 32 : (r + 1) * 32].reshape(BLOCK, 128).astype(BF16)
    copies = []
    for i in range(1, GX):
        device = peers[i - 1]
        copies.append(remote(outbox.at[device[0]], inbox.at[gx], send_sem.at[i - 1], recv_sem.at[i - 1], device))
    for copy in copies:
        copy.start()
    inbox[gx] = outbox[gx]
    for i in range(1, GX):
        there = inbox.at[lax.rem(gx + GX - i, GX)]
        remote(there, there, send_sem.at[i - 1], recv_sem.at[i - 1], peers[GX - 1 - i]).wait_recv()
    for f in range(4):
        low = inbox[2 * f].astype(F32).reshape(32, 8, 128)
        high = inbox[2 * f + 1].astype(F32).reshape(32, 8, 128)
        core[:, f] = jnp.concatenate([low, high], axis=1).astype(BF16)
    for copy in copies:
        copy.wait_send()


def core_of(basis_t, rows):
    return pl.pallas_call(
        core_kernel,
        out_shape=jax.ShapeDtypeStruct((32, 4, 16, 128), BF16),
        in_specs=[pl.BlockSpec(memory_space=VMEM)] * 2,
        out_specs=pl.BlockSpec(memory_space=VMEM),
        scratch_shapes=[
            VMEM((BLOCK, 8, 128), F32),
            VMEM((GX, BLOCK, 128), BF16),
            VMEM((GX, BLOCK, 128), BF16),
            pltpu.SemaphoreType.DMA((7,)),
            pltpu.SemaphoreType.DMA((7,)),
        ],
        compiler_params=pltpu.CompilerParams(collective_id=2, has_side_effects=True, vmem_limit_bytes=LIMIT),
        name="core",
    )(basis_t, rows)


PANEL = 64
EXACT = lax.Precision.HIGHEST


def split(value):
    high = value.astype(BF16)
    return high, (value - high.astype(F32)).astype(BF16)


def eliminate(block):
    count = PANEL // 8
    line = lax.broadcasted_iota(jnp.int32, (8, 128), 0)
    lane = lax.broadcasted_iota(jnp.int32, (8, 128), 1)
    tiles = [jnp.where(lane == line + 8 * i, 1.0, block[8 * i : 8 * i + 8]) for i in range(count)]
    for g in range(count):
        first = PANEL + 8 * g
        spread = [[jnp.broadcast_to(tiles[i][:, first + t : first + t + 1], (8, 128)) for t in range(8)] for i in range(g, count)]
        scale = jnp.zeros((8, 128), F32)
        for t in range(8):
            pivot = jnp.broadcast_to(spread[0][t][t : t + 1], (8, 128))
            inverse = 1.0 / pivot
            scale = jnp.where(line == t, lax.rsqrt(pivot), scale)
            row = jnp.broadcast_to(tiles[g][t : t + 1], (8, 128))
            heads = [jnp.broadcast_to(spread[0][u][t : t + 1], (8, 128)) for u in range(t + 1, 8)]
            for n, i in enumerate(range(g, count)):
                factor = spread[n][t] * inverse
                if n == 0:
                    factor = jnp.where(line > t, factor, 0.0)
                tiles[i] = tiles[i] - factor * row
                for u in range(t + 1, 8):
                    spread[n][u] = spread[n][u] - factor * heads[u - t - 1]
        tiles[g] = tiles[g] * scale
    return jnp.concatenate(tiles, axis=0)


def invert_factor(work):
    for k in range(BLOCK // PANEL):
        here = slice(k * PANEL, (k + 1) * PANEL)
        base = (k // 2) * 128
        both = work[here, base : base + 128]
        if k % 2 == 0:
            both = pltpu.roll(both, PANEL, 1)
        lane = lax.broadcasted_iota(jnp.int32, both.shape, 1)
        small = eliminate(jnp.where(lane < PANEL, 0.0, both))[:, :PANEL]
        left, right = base, BLOCK + (k // 2 + 1) * 128
        rows = jnp.dot(small, work[here, left:right], precision=EXACT, preferred_element_type=F32)
        work[here, left:right] = rows
        if k + 1 < BLOCK // PANEL:
            below = (k + 1) * PANEL
            factor = rows[:, below - left : BLOCK - left]
            work[below:, left:right] = work[below:, left:right] - lax.dot_general(
                factor, rows, (((0,), (0,)), ((), ())), precision=EXACT, preferred_element_type=F32
            )


def iterate_kernel(blocks, start, basis, rounded, high_g, low_g, parts, image, current, work):
    gx = lax.axis_index("gx")

    def spread(s, _):
        j = s % 8
        i = (j + s // 8) % 8
        block = blocks[pl.ds(pl.multiple_of(s * BLOCK, BLOCK), BLOCK), :]
        for row, column, value in ((j, i, block), (i, j, block.T)):
            high, low = split(value)
            high_g[column, pl.ds(pl.multiple_of(row * BLOCK, BLOCK), BLOCK), :] = high
            low_g[column, pl.ds(pl.multiple_of(row * BLOCK, BLOCK), BLOCK), :] = low
        return 0

    lax.fori_loop(0, PAIRS, spread, 0)

    def columns(j):
        return pl.ds(pl.multiple_of(j * BLOCK, BLOCK), BLOCK)

    def keep(j, value):
        high, low = split(value)
        parts[0:BLOCK, columns(j)] = high
        parts[BLOCK:, columns(j)] = low

    def load(j, _):
        keep(j, start[columns(j), :].T)
        return 0

    lax.fori_loop(0, GX, load, 0)
    unit = jnp.where(
        lax.broadcasted_iota(jnp.int32, (BLOCK, BLOCK), 0) == lax.broadcasted_iota(jnp.int32, (BLOCK, BLOCK), 1), 1.0, 0.0
    )

    def iteration(_, carry):
        work[:, 0:BLOCK] = jnp.zeros((BLOCK, BLOCK), F32)
        work[:, BLOCK:] = unit

        def multiply(j, _):
            both = jnp.dot(parts[...], high_g[j], preferred_element_type=F32)
            value = both[:BLOCK] + (both[BLOCK:] + jnp.dot(parts[0:BLOCK, :], low_g[j], preferred_element_type=F32))
            image[:, columns(j)] = value
            work[:, 0:BLOCK] += lax.dot_general(
                value, value, (((1,), (1,)), ((), ())), precision=EXACT, preferred_element_type=F32
            )
            return 0

        lax.fori_loop(0, GX, multiply, 0)
        invert_factor(work)

        def apply(j, _):
            value = jnp.dot(work[:, BLOCK:], image[:, columns(j)], precision=EXACT, preferred_element_type=F32)
            current[:, columns(j)] = value
            keep(j, value)
            return 0

        lax.fori_loop(0, GX, apply, 0)
        return carry

    lax.fori_loop(0, ITERS, iteration, 0)
    basis[...] = current[:, columns(gx)].T
    rounded[...] = parts[0:BLOCK, :]


def iterate(blocks, start):
    return pl.pallas_call(
        iterate_kernel,
        out_shape=(jax.ShapeDtypeStruct((BLOCK, BLOCK), F32), jax.ShapeDtypeStruct((BLOCK, GX * BLOCK), BF16)),
        in_specs=[pl.BlockSpec(memory_space=VMEM)] * 2,
        out_specs=(pl.BlockSpec(memory_space=VMEM),) * 2,
        scratch_shapes=[
            VMEM((GX, GX * BLOCK, BLOCK), BF16),
            VMEM((GX, GX * BLOCK, BLOCK), BF16),
            VMEM((2 * BLOCK, GX * BLOCK), BF16),
            VMEM((BLOCK, GX * BLOCK), F32),
            VMEM((BLOCK, GX * BLOCK), F32),
            VMEM((BLOCK, 2 * BLOCK), F32),
        ],
        compiler_params=pltpu.CompilerParams(vmem_limit_bytes=LIMIT),
        name="iterate",
    )(blocks, start)


def per_device(wind_field, terrain, start_basis):
    basis = lax.all_gather(start_basis, "gx", axis=0, tiled=True)
    advanced, rows = step(wind_field, terrain)
    basis_rows, rounded = iterate(gram_blocks(rows), basis)
    core = core_of(rounded, rows)
    return (advanced, basis_rows, core)


def solution(mesh):
    placed = (P("ft", None, "gx", "gy"), P("gx", "gy"), P("gx", None))
    return jax.shard_map(
        per_device,
        mesh=mesh,
        in_specs=placed,
        out_specs=(P("ft", None, "gx", "gy"), P("gx", None), P("gx", "ft", None, "gy")),
        check_vma=False,
    )
```

```python
import functools

import jax
import jax.numpy as jnp
from jax import lax
from jax.experimental import pallas as pl
from jax.experimental.pallas import tpu as pltpu
from jax.sharding import PartitionSpec as P

ITERS = 4
MESH = pl.DeviceIdType.MESH
VMEM = pltpu.VMEM
F32 = jnp.float32
BF16 = jnp.bfloat16
GX = 8
BLOCK = 256
PAIRS = 36
LIMIT = 56 * 1024 * 1024

diffusion_number = 0.15


def place():
    return lax.axis_index("gx"), lax.axis_index("gy"), lax.axis_index("ft")


def greet(devices):
    barrier = pltpu.get_barrier_semaphore()
    for device in devices:
        pl.semaphore_signal(barrier, inc=1, device_id=device, device_id_type=MESH)
    pl.semaphore_wait(barrier, len(devices))


def remote(src, dst, send, recv, device):
    return pltpu.make_async_remote_copy(
        src_ref=src, dst_ref=dst, send_sem=send, recv_sem=recv, device_id=device, device_id_type=MESH
    )


HALF = 18 * BLOCK
PART = HALF // 3


def gram_kernel(
    wind, terrain, start, advanced, rows, gram, basis,
    edge_out, edge_in, line_out, line_in, merged, near_x, near_y,
    partial, half_in, in_1, in_2, in_3,
    halo_send, halo_recv, send_sem, recv_sem, own_sem, basis_send, basis_recv, basis_own,
    pair_send, pair_recv, send_1, recv_1, send_2, recv_2, send_3, recv_3,
    back_3, home_3, back_2, home_2, back_1, home_1, last_send, last_recv,
):
    gx, gy, ft = place()
    core, z_hi = ft % 2, ft // 2
    coords = (gy, gx // 2, z_hi * 2 + gx % 2)

    def at(axis, t):
        if axis == 0:
            return (gx, t, ft)
        if axis == 1:
            return (t * 2 + gx % 2, gy, ft)
        return ((gx // 2) * 2 + t % 2, gy, (t // 2) * 2 + core)

    def peer(axis, o):
        t = lax.rem(coords[axis] + o, 4)
        return t, at(axis, t)

    peers = [(lax.rem(gx + i, GX), gy, ft) for i in range(1, GX)]
    sides = [(gx, lax.rem(gy + o, 4), ft) for o in range(1, 4)]
    sibling = (gx, gy, z_hi * 2 + 1 - core)
    far = (gx, gy, lax.rem(ft + 2, 4))
    far_odd = ((gx // 2) * 2 + 1 - gx % 2, gy, lax.rem(ft + 2, 4))
    greet(peers + sides + [sibling, far, far_odd])

    def basis_rows(first, count):
        return basis.at[:, pl.ds(pl.multiple_of(first, 16), count)]

    piece = (core * 8 + gy * 2 + z_hi) * 16
    here = pl.ds(pl.multiple_of(piece, 16), 16)
    basis_copies = [
        remote(start.at[here], basis.at[gx, here], basis_send.at[n], basis_recv.at[n], device) for n, device in enumerate(peers)
    ]
    for copy in basis_copies:
        copy.start()
    own_basis = pltpu.make_async_copy(start.at[here], basis.at[gx, here], basis_own)
    own_basis.start()

    lane = lax.broadcasted_iota(jnp.int32, (BLOCK, 128), 1)
    line = lax.broadcasted_iota(jnp.int32, (BLOCK, 128), 0)

    def collect(k, packed):
        tile = wind[k // 16, k % 16].astype(F32)
        line_out[0, pl.ds(k, 1), :] = tile[0:1]
        line_out[1, pl.ds(k, 1), :] = tile[BLOCK - 1 : BLOCK]
        return jnp.where(lane // 2 == k, pltpu.roll(tile, 2 * k + 1, 1), packed)

    packed = lax.fori_loop(0, 64, collect, jnp.zeros((BLOCK, 128), F32))
    edge_out[...] = packed.astype(BF16)
    halos = [
        remote(line_out.at[1], line_in.at[0], halo_send.at[0], halo_recv.at[0], peers[0]),
        remote(line_out.at[0], line_in.at[1], halo_send.at[1], halo_recv.at[1], peers[6]),
        remote(edge_out, edge_in.at[0], halo_send.at[2], halo_recv.at[2], sides[0]),
        remote(edge_out, edge_in.at[1], halo_send.at[3], halo_recv.at[3], sides[2]),
    ]
    for copy in halos:
        copy.start()
    a = lax.broadcasted_iota(jnp.int32, (BLOCK, BLOCK), 0)
    b = lax.broadcasted_iota(jnp.int32, (BLOCK, BLOCK), 1)
    near_x[...] = jnp.where(jnp.abs(a - b) == 1, 1.0, 0.0).astype(BF16)
    near_y[...] = near_x[0:128, 0:128]
    for copy in halos:
        copy.wait()
    from_before = pltpu.roll(edge_in[0].astype(F32), 1, 1)
    from_after = pltpu.roll(edge_in[1].astype(F32), 127, 1)
    merged[...] = jnp.where(lane % 2 == 0, from_after, from_before)

    def chunk(c):
        field, first = c // 2, (c % 2) * 8

        def level(i, _):
            z = first + i
            k = field * 16 + z
            tile = wind[field, z]
            center = tile.astype(F32)
            above = wind[field, lax.rem(z + 1, 16)].astype(F32)
            below = wind[field, lax.rem(z + 15, 16)].astype(F32)
            around = jnp.where(z < 15, above, 0.0) + jnp.where(z > 0, below, 0.0)
            around += jnp.dot(near_x[...], tile, preferred_element_type=F32)
            around += jnp.dot(tile, near_y[...], preferred_element_type=F32)
            side = pltpu.roll(merged[...], 127 - 2 * k, 1)
            around += jnp.where((lane == 0) | (lane == 127), side, 0.0)
            around += jnp.where(line == 0, line_in[0, pl.ds(k, 1), :], 0.0)
            around += jnp.where(line == BLOCK - 1, line_in[1, pl.ds(k, 1), :], 0.0)
            stepped = center + diffusion_number * (around - 6.0 * center)
            advanced[field, z] = jnp.where(z >= terrain[...], stepped, 0.0).astype(BF16)
            return 0

        lax.fori_loop(0, 8, level, 0)
        return advanced.at[field, pl.ds(first, 8)]

    def to_peer(i):
        c = lax.rem(gx + i, GX)
        part = advanced.at[c // 2, pl.ds((c % 2) * 8, 8)]
        return remote(part, rows.at[gx], send_sem.at[i - 1], recv_sem.at[i - 1], (c, gy, ft))

    def send_one(i, _):
        chunk(lax.rem(gx + i, GX))
        to_peer(i).start()
        return 0

    lax.fori_loop(1, 3, send_one, 0)
    own_basis.wait()
    for copy in basis_copies:
        copy.wait()
    spread_far = remote(basis_rows(piece, 16), basis_rows(piece, 16), basis_send.at[7], basis_recv.at[7], far)
    spread_far.start()
    lax.fori_loop(3, 5, send_one, 0)
    spread_far.wait()
    two = piece - z_hi * 16
    spread_sides = [
        remote(basis_rows(two, 32), basis_rows(two, 32), basis_send.at[8 + n], basis_recv.at[8 + n], device)
        for n, device in enumerate(sides)
    ]
    for copy in spread_sides:
        copy.start()
    lax.fori_loop(5, GX, send_one, 0)
    own = pltpu.make_async_copy(chunk(gx), rows.at[gx], own_sem)
    own.start()
    own.wait()

    def store(s):
        return pl.ds(pl.multiple_of(((s % 2) * 18 + s // 2) * BLOCK, BLOCK), BLOCK)

    def block(s):
        j = s % 8
        i = (j + s // 8) % 8
        left = jnp.concatenate([rows[j, z] for z in range(8)], axis=1)
        right = jnp.concatenate([rows[i, z] for z in range(8)], axis=1)
        partial[store(s), :] = lax.dot_general(left, right, (((1,), (1,)), ((), ())), preferred_element_type=F32)

        @pl.when(s % 2 != core)
        def _():
            swap(s // 2).start()

    def swap(n):
        src = partial.at[pl.ds(pl.multiple_of(((1 - core) * 18 + n) * BLOCK, BLOCK), BLOCK)]
        return remote(src, half_in.at[n], pair_send.at[n], pair_recv.at[n], sibling)

    for i in range(GX):
        source = lax.rem(gx + GX - i, GX)
        if i > 0:
            there = rows.at[source]
            remote(there, there, send_sem.at[i - 1], recv_sem.at[i - 1], (source, gy, ft)).wait_recv()
        lax.fori_loop(0, min(i, 3) + 1, lambda d, _: (block(d * 8 + source), 0)[1], 0)
        if i >= 4:
            block(32 + source % 4)
        if i >= 5:
            lax.fori_loop(5, i + 1, lambda d, _: (block((8 - d) * 8 + (source + d) % 8), 0)[1], 0)
    for copy in spread_sides:
        copy.wait()
    eight = core * 128
    spread_pair = remote(basis_rows(eight, 128), basis_rows(eight, 128), basis_send.at[11], basis_recv.at[11], sibling)

    mine = pl.multiple_of(core * HALF, HALF)
    other = pl.multiple_of((1 - core) * HALF, HALF)

    def take(n, _):
        swap(n).wait()
        here = pl.ds(pl.multiple_of(mine + n * BLOCK, BLOCK), BLOCK)
        partial[here, :] = partial[here, :] + half_in[n]
        return 0

    lax.fori_loop(0, 18, take, 0)
    spread_pair.start()

    def add(first, count, sources, tile):
        def body(k, _):
            here = pl.ds(pl.multiple_of(first + k * tile, 8), tile)
            there = pl.ds(pl.multiple_of(k * tile, 8), tile)
            total = partial[here, :]
            for source in sources:
                total = total + source[there, :]
            partial[here, :] = total
            return 0

        lax.fori_loop(0, count // tile, body, 0)

    starts = [[mine + p * PART] for p in range(3)]
    sizes = [PART // 4, PART // 16, PART // 64]
    for depth, (inbox, send, recv) in enumerate(((in_1, send_1, recv_1), (in_2, send_2, recv_2), (in_3, send_3, recv_3))):
        size = sizes[depth]
        copies = []
        for p in range(3):
            axis = (p + depth) % 3
            for o in range(1, 4):
                t, device = peer(axis, o)
                src = pl.ds(pl.multiple_of(starts[p][depth] + t * size, 8), size)
                n = p * 3 + o - 1
                copies.append(remote(partial.at[src], inbox.at[n], send.at[n], recv.at[n], device))
        for copy in copies:
            copy.start()
        for copy in copies:
            copy.wait()
        for p in range(3):
            first = starts[p][depth] + coords[(p + depth) % 3] * size
            starts[p].append(first)
            add(first, size, [inbox.at[p * 3 + o] for o in range(3)], min(size, 96))

    for p in range(3):
        here = pl.ds(pl.multiple_of(starts[p][3], 8), sizes[2])
        gram[here, :] = partial[here, :]
    lasts = []

    def pass_on(p, first, n):
        here = gram.at[pl.ds(pl.multiple_of(first, 8), sizes[0])]
        copy = remote(here, here, last_send.at[n], last_recv.at[n], sibling)
        copy.start()
        lasts.append(copy)

    for depth, send, recv in ((2, back_3, home_3), (1, back_2, home_2), (0, back_1, home_1)):
        size = sizes[depth]
        copies = []
        for p in range(3):
            here = gram.at[pl.ds(pl.multiple_of(starts[p][depth + 1], 8), size)]
            for o in range(1, 4):
                _, device = peer((p + depth) % 3, o)
                n = p * 3 + o - 1
                copies.append(remote(here, here, send.at[n], recv.at[n], device))
        for copy in copies:
            copy.start()
        if depth == 0:
            for p in range(3):
                pass_on(p, starts[p][1], p * 4)
        for p in range(3):
            axis = (p + depth) % 3
            for o in range(1, 4):
                n = p * 3 + o - 1
                t, device = peer(axis, 4 - o)
                first = starts[p][depth] + t * size
                there = gram.at[pl.ds(pl.multiple_of(first, 8), size)]
                remote(there, there, send.at[n], recv.at[n], device).wait_recv()
                if depth == 0:
                    pass_on(p, first, p * 4 + o)
        for copy in copies:
            copy.wait_send()
    for p in range(3):
        for o in range(4):
            n = p * 4 + o
            t = lax.rem(coords[p] + 4 - o, 4)
            there = gram.at[pl.ds(pl.multiple_of(other + p * PART + t * sizes[0], 8), sizes[0])]
            remote(there, there, last_send.at[n], last_recv.at[n], sibling).wait_recv()
    for copy in lasts:
        copy.wait_send()
    spread_pair.wait()

    def wait_sent(i, _):
        to_peer(i).wait_send()
        return 0

    lax.fori_loop(1, GX, wait_sent, 0)


def step_and_gram(wind_field, terrain, start_basis):
    dma = pltpu.SemaphoreType.DMA
    return pl.pallas_call(
        gram_kernel,
        out_shape=(
            jax.ShapeDtypeStruct((4, 16, BLOCK, 128), BF16),
            jax.ShapeDtypeStruct((GX, 8, BLOCK, 128), BF16),
            jax.ShapeDtypeStruct((PAIRS * BLOCK, BLOCK), F32),
            jax.ShapeDtypeStruct((GX, BLOCK, BLOCK), F32),
        ),
        in_specs=[pl.BlockSpec(memory_space=VMEM)] * 3,
        out_specs=(pl.BlockSpec(memory_space=VMEM),) * 4,
        scratch_shapes=[
            VMEM((BLOCK, 128), BF16),
            VMEM((2, BLOCK, 128), BF16),
            VMEM((2, 64, 128), F32),
            VMEM((2, 64, 128), F32),
            VMEM((BLOCK, 128), F32),
            VMEM((BLOCK, BLOCK), BF16),
            VMEM((128, 128), BF16),
            VMEM((PAIRS * BLOCK, BLOCK), F32),
            VMEM((18, BLOCK, BLOCK), F32),
            VMEM((9, PART // 4, BLOCK), F32),
            VMEM((9, PART // 16, BLOCK), F32),
            VMEM((9, PART // 64, BLOCK), F32),
            dma((4,)), dma((4,)), dma((7,)), dma((7,)), dma, dma((12,)), dma((12,)), dma,
            dma((18,)), dma((18,)),
        ]
        + [dma((9,))] * 12
        + [dma((12,))] * 2,
        compiler_params=pltpu.CompilerParams(collective_id=0, has_side_effects=True, vmem_limit_bytes=LIMIT),
        name="step_and_gram",
    )(wind_field, terrain, start_basis)


def core_kernel(basis_t, rows, core, stage, outbox, inbox, send_sem, recv_sem):
    gx, gy, ft = place()
    peers = [(lax.rem(gx + i, GX), gy, ft) for i in range(1, GX)]
    greet(peers)
    for z in range(0, 8, 2):
        total = jnp.zeros((BLOCK, BLOCK), F32)
        for j in range(GX):
            pair = jnp.concatenate([rows[j, z], rows[j, z + 1]], axis=1)
            total += jnp.dot(basis_t[:, j * BLOCK : (j + 1) * BLOCK], pair, preferred_element_type=F32)
        stage[:, z, :] = total[:, :128]
        stage[:, z + 1, :] = total[:, 128:]
    for r in range(GX):
        outbox[r] = stage[r * 32 : (r + 1) * 32].reshape(BLOCK, 128).astype(BF16)
    copies = []
    for i in range(1, GX):
        device = peers[i - 1]
        copies.append(remote(outbox.at[device[0]], inbox.at[gx], send_sem.at[i - 1], recv_sem.at[i - 1], device))
    for copy in copies:
        copy.start()
    inbox[gx] = outbox[gx]
    for i in range(1, GX):
        there = inbox.at[lax.rem(gx + GX - i, GX)]
        remote(there, there, send_sem.at[i - 1], recv_sem.at[i - 1], peers[GX - 1 - i]).wait_recv()
    for f in range(4):
        low = inbox[2 * f].astype(F32).reshape(32, 8, 128)
        high = inbox[2 * f + 1].astype(F32).reshape(32, 8, 128)
        core[:, f] = jnp.concatenate([low, high], axis=1).astype(BF16)
    for copy in copies:
        copy.wait_send()


def core_of(basis_t, rows):
    return pl.pallas_call(
        core_kernel,
        out_shape=jax.ShapeDtypeStruct((32, 4, 16, 128), BF16),
        in_specs=[pl.BlockSpec(memory_space=VMEM)] * 2,
        out_specs=pl.BlockSpec(memory_space=VMEM),
        scratch_shapes=[
            VMEM((BLOCK, 8, 128), F32),
            VMEM((GX, BLOCK, 128), BF16),
            VMEM((GX, BLOCK, 128), BF16),
            pltpu.SemaphoreType.DMA((7,)),
            pltpu.SemaphoreType.DMA((7,)),
        ],
        compiler_params=pltpu.CompilerParams(collective_id=1, has_side_effects=True, vmem_limit_bytes=LIMIT),
        name="core",
    )(basis_t, rows)


PANEL = 64
EXACT = lax.Precision.HIGHEST


def split(value):
    high = value.astype(BF16)
    return high, (value - high.astype(F32)).astype(BF16)


def eliminate(block):
    count = PANEL // 8
    line = lax.broadcasted_iota(jnp.int32, (8, 128), 0)
    lane = lax.broadcasted_iota(jnp.int32, (8, 128), 1)
    tiles = [jnp.where(lane == line + 8 * i, 1.0, block[8 * i : 8 * i + 8]) for i in range(count)]
    for g in range(count):
        first = PANEL + 8 * g
        spread = [[jnp.broadcast_to(tiles[i][:, first + t : first + t + 1], (8, 128)) for t in range(8)] for i in range(g, count)]
        scale = jnp.zeros((8, 128), F32)
        for t in range(8):
            pivot = jnp.broadcast_to(spread[0][t][t : t + 1], (8, 128))
            inverse = 1.0 / pivot
            scale = jnp.where(line == t, lax.rsqrt(pivot), scale)
            row = jnp.broadcast_to(tiles[g][t : t + 1], (8, 128))
            heads = [jnp.broadcast_to(spread[0][u][t : t + 1], (8, 128)) for u in range(t + 1, 8)]
            for n, i in enumerate(range(g, count)):
                factor = spread[n][t] * inverse
                if n == 0:
                    factor = jnp.where(line > t, factor, 0.0)
                tiles[i] = tiles[i] - factor * row
                for u in range(t + 1, 8):
                    spread[n][u] = spread[n][u] - factor * heads[u - t - 1]
        tiles[g] = tiles[g] * scale
    return jnp.concatenate(tiles, axis=0)


def invert_factor(work):
    for k in range(BLOCK // PANEL):
        here = slice(k * PANEL, (k + 1) * PANEL)
        base = (k // 2) * 128
        both = work[here, base : base + 128]
        if k % 2 == 0:
            both = pltpu.roll(both, PANEL, 1)
        lane = lax.broadcasted_iota(jnp.int32, both.shape, 1)
        small = eliminate(jnp.where(lane < PANEL, 0.0, both))[:, :PANEL]
        left, right = base, BLOCK + (k // 2 + 1) * 128
        rows = jnp.dot(small, work[here, left:right], precision=EXACT, preferred_element_type=F32)
        work[here, left:right] = rows
        if k + 1 < BLOCK // PANEL:
            below = (k + 1) * PANEL
            factor = rows[:, below - left : BLOCK - left]
            work[below:, left:right] = work[below:, left:right] - lax.dot_general(
                factor, rows, (((0,), (0,)), ((), ())), precision=EXACT, preferred_element_type=F32
            )


def iterate_kernel(blocks, start, basis, rounded, high_g, low_g, parts, image, current, work):
    gx = lax.axis_index("gx")

    def spread(n, _):
        s = (n % 18) * 2 + n // 18
        j = s % 8
        i = (j + s // 8) % 8
        block = blocks[pl.ds(pl.multiple_of(n * BLOCK, BLOCK), BLOCK), :]
        for row, column, value in ((j, i, block), (i, j, block.T)):
            high, low = split(value)
            high_g[column, pl.ds(pl.multiple_of(row * BLOCK, BLOCK), BLOCK), :] = high
            low_g[column, pl.ds(pl.multiple_of(row * BLOCK, BLOCK), BLOCK), :] = low
        return 0

    lax.fori_loop(0, PAIRS, spread, 0)

    def columns(j):
        return pl.ds(pl.multiple_of(j * BLOCK, BLOCK), BLOCK)

    def keep(j, value):
        high, low = split(value)
        parts[0:BLOCK, columns(j)] = high
        parts[BLOCK:, columns(j)] = low

    def load(j, _):
        keep(j, start[j].T)
        return 0

    lax.fori_loop(0, GX, load, 0)
    unit = jnp.where(
        lax.broadcasted_iota(jnp.int32, (BLOCK, BLOCK), 0) == lax.broadcasted_iota(jnp.int32, (BLOCK, BLOCK), 1), 1.0, 0.0
    )

    def iteration(_, carry):
        work[:, 0:BLOCK] = jnp.zeros((BLOCK, BLOCK), F32)
        work[:, BLOCK:] = unit

        def multiply(j, _):
            both = jnp.dot(parts[...], high_g[j], preferred_element_type=F32)
            value = both[:BLOCK] + (both[BLOCK:] + jnp.dot(parts[0:BLOCK, :], low_g[j], preferred_element_type=F32))
            image[:, columns(j)] = value
            work[:, 0:BLOCK] += lax.dot_general(
                value, value, (((1,), (1,)), ((), ())), precision=EXACT, preferred_element_type=F32
            )
            return 0

        lax.fori_loop(0, GX, multiply, 0)
        invert_factor(work)

        def apply(j, _):
            value = jnp.dot(work[:, BLOCK:], image[:, columns(j)], precision=EXACT, preferred_element_type=F32)
            current[:, columns(j)] = value
            keep(j, value)
            return 0

        lax.fori_loop(0, GX, apply, 0)
        return carry

    lax.fori_loop(0, ITERS, iteration, 0)
    basis[...] = current[:, columns(gx)].T
    rounded[...] = parts[0:BLOCK, :]


def iterate(blocks, start):
    return pl.pallas_call(
        iterate_kernel,
        out_shape=(jax.ShapeDtypeStruct((BLOCK, BLOCK), F32), jax.ShapeDtypeStruct((BLOCK, GX * BLOCK), BF16)),
        in_specs=[pl.BlockSpec(memory_space=VMEM)] * 2,
        out_specs=(pl.BlockSpec(memory_space=VMEM),) * 2,
        scratch_shapes=[
            VMEM((GX, GX * BLOCK, BLOCK), BF16),
            VMEM((GX, GX * BLOCK, BLOCK), BF16),
            VMEM((2 * BLOCK, GX * BLOCK), BF16),
            VMEM((BLOCK, GX * BLOCK), F32),
            VMEM((BLOCK, GX * BLOCK), F32),
            VMEM((BLOCK, 2 * BLOCK), F32),
        ],
        compiler_params=pltpu.CompilerParams(vmem_limit_bytes=LIMIT),
        name="iterate",
    )(blocks, start)


def per_device(wind_field, terrain, start_basis):
    advanced, rows, blocks, basis = step_and_gram(wind_field, terrain, start_basis)
    basis_rows, rounded = iterate(blocks, basis)
    core = core_of(rounded, rows)
    return (advanced, basis_rows, core)


def solution(mesh):
    placed = (P("ft", None, "gx", "gy"), P("gx", "gy"), P("gx", None))
    return jax.shard_map(
        per_device,
        mesh=mesh,
        in_specs=placed,
        out_specs=(P("ft", None, "gx", "gy"), P("gx", None), P("gx", "ft", None, "gy")),
        check_vma=False,
    )
```

```python
import functools

import jax
import jax.numpy as jnp
from jax import lax
from jax.experimental import pallas as pl
from jax.experimental.pallas import tpu as pltpu
from jax.sharding import PartitionSpec as P

ITERS = 4
MESH = pl.DeviceIdType.MESH
VMEM = pltpu.VMEM
F32 = jnp.float32
BF16 = jnp.bfloat16
GX = 8
BLOCK = 256
PAIRS = 36
LIMIT = 56 * 1024 * 1024

diffusion_number = 0.15


def place():
    return lax.axis_index("gx"), lax.axis_index("gy"), lax.axis_index("ft")


def greet(devices):
    barrier = pltpu.get_barrier_semaphore()
    for device in devices:
        pl.semaphore_signal(barrier, inc=1, device_id=device, device_id_type=MESH)
    pl.semaphore_wait(barrier, len(devices))


def remote(src, dst, send, recv, device):
    return pltpu.make_async_remote_copy(
        src_ref=src, dst_ref=dst, send_sem=send, recv_sem=recv, device_id=device, device_id_type=MESH
    )


HALF = 18 * BLOCK
PART = HALF // 3


def gram_kernel(
    wind, terrain, start, advanced, rows, gram, basis,
    edge_out, edge_in, line_out, line_in, merged, near_x, near_y,
    relay, partial, half_in, in_1, in_2, in_3,
    halo_send, halo_recv, send_sem, recv_sem, relay_send, relay_recv, own_sem, basis_send, basis_recv, basis_own,
    pair_send, pair_recv, send_1, recv_1, send_2, recv_2, send_3, recv_3,
    back_3, home_3, back_2, home_2, back_1, home_1, last_send, last_recv,
):
    gx, gy, ft = place()
    core, z_hi = ft % 2, ft // 2
    coords = (gy, gx // 2, z_hi * 2 + gx % 2)

    def at(axis, t):
        if axis == 0:
            return (gx, t, ft)
        if axis == 1:
            return (t * 2 + gx % 2, gy, ft)
        return ((gx // 2) * 2 + t % 2, gy, (t // 2) * 2 + core)

    def peer(axis, o):
        t = lax.rem(coords[axis] + o, 4)
        return t, at(axis, t)

    y, z_lo = gx // 2, gx % 2
    beside = (y * 2 + 1 - z_lo, gy, ft)
    peers = [(lax.rem(gx + i, GX), gy, ft) for i in range(1, GX)]
    sides = [(gx, lax.rem(gy + o, 4), ft) for o in range(1, 4)]
    sibling = (gx, gy, z_hi * 2 + 1 - core)
    far = (gx, gy, lax.rem(ft + 2, 4))
    far_odd = ((gx // 2) * 2 + 1 - gx % 2, gy, lax.rem(ft + 2, 4))
    greet(peers + sides + [sibling, far, far_odd])

    def basis_rows(first, count):
        return basis.at[:, pl.ds(pl.multiple_of(first, 16), count)]

    piece = (core * 8 + gy * 2 + z_hi) * 16
    here = pl.ds(pl.multiple_of(piece, 16), 16)
    basis_copies = [
        remote(start.at[here], basis.at[gx, here], basis_send.at[n], basis_recv.at[n], device) for n, device in enumerate(peers)
    ]
    for copy in basis_copies:
        copy.start()
    own_basis = pltpu.make_async_copy(start.at[here], basis.at[gx, here], basis_own)
    own_basis.start()

    lane = lax.broadcasted_iota(jnp.int32, (BLOCK, 128), 1)
    line = lax.broadcasted_iota(jnp.int32, (BLOCK, 128), 0)

    def collect(k, packed):
        tile = wind[k // 16, k % 16].astype(F32)
        line_out[0, pl.ds(k, 1), :] = tile[0:1]
        line_out[1, pl.ds(k, 1), :] = tile[BLOCK - 1 : BLOCK]
        return jnp.where(lane // 2 == k, pltpu.roll(tile, 2 * k + 1, 1), packed)

    packed = lax.fori_loop(0, 64, collect, jnp.zeros((BLOCK, 128), F32))
    edge_out[...] = packed.astype(BF16)
    halos = [
        remote(line_out.at[1], line_in.at[0], halo_send.at[0], halo_recv.at[0], peers[0]),
        remote(line_out.at[0], line_in.at[1], halo_send.at[1], halo_recv.at[1], peers[6]),
        remote(edge_out, edge_in.at[0], halo_send.at[2], halo_recv.at[2], sides[0]),
        remote(edge_out, edge_in.at[1], halo_send.at[3], halo_recv.at[3], sides[2]),
    ]
    for copy in halos:
        copy.start()
    a = lax.broadcasted_iota(jnp.int32, (BLOCK, BLOCK), 0)
    b = lax.broadcasted_iota(jnp.int32, (BLOCK, BLOCK), 1)
    near_x[...] = jnp.where(jnp.abs(a - b) == 1, 1.0, 0.0).astype(BF16)
    near_y[...] = near_x[0:128, 0:128]
    for copy in halos:
        copy.wait()
    from_before = pltpu.roll(edge_in[0].astype(F32), 1, 1)
    from_after = pltpu.roll(edge_in[1].astype(F32), 127, 1)
    merged[...] = jnp.where(lane % 2 == 0, from_after, from_before)

    def chunk(c):
        field, first = c // 2, (c % 2) * 8

        def level(i, _):
            z = first + i
            k = field * 16 + z
            tile = wind[field, z]
            center = tile.astype(F32)
            above = wind[field, lax.rem(z + 1, 16)].astype(F32)
            below = wind[field, lax.rem(z + 15, 16)].astype(F32)
            around = jnp.where(z < 15, above, 0.0) + jnp.where(z > 0, below, 0.0)
            around += jnp.dot(near_x[...], tile, preferred_element_type=F32)
            around += jnp.dot(tile, near_y[...], preferred_element_type=F32)
            side = pltpu.roll(merged[...], 127 - 2 * k, 1)
            around += jnp.where((lane == 0) | (lane == 127), side, 0.0)
            around += jnp.where(line == 0, line_in[0, pl.ds(k, 1), :], 0.0)
            around += jnp.where(line == BLOCK - 1, line_in[1, pl.ds(k, 1), :], 0.0)
            stepped = center + diffusion_number * (around - 6.0 * center)
            advanced[field, z] = jnp.where(z >= terrain[...], stepped, 0.0).astype(BF16)
            return 0

        lax.fori_loop(0, 8, level, 0)
        return advanced.at[field, pl.ds(first, 8)]

    def send(n, dy, dz):
        c = lax.rem(y + dy, 4) * 2 + lax.rem(z_lo + dz, 2)
        part = advanced.at[c // 2, pl.ds((c % 2) * 8, 8)]
        if dz == 1 and dy > 0:
            return remote(part, relay.at[dy - 1], send_sem.at[n], relay_recv.at[dy - 1], beside)
        return remote(part, rows.at[gx], send_sem.at[n], recv_sem.at[dy * 2 + dz - 1], (c, gy, ft))

    def pass_along(dy):
        arrived = relay.at[dy - 1]
        remote(arrived, arrived, relay_send.at[dy - 1], relay_recv.at[dy - 1], beside).wait_recv()
        target = (lax.rem(y + dy, 4) * 2 + z_lo, gy, ft)
        copy = remote(arrived, rows.at[beside[0]], relay_send.at[dy - 1], recv_sem.at[dy * 2], target)
        copy.start()
        sent.append(copy)

    sent = []
    for n, (dy, dz) in enumerate(((2, 1), (1, 0), (1, 1), (3, 0), (3, 1), (2, 0), (0, 1))):
        chunk(lax.rem(y + dy, 4) * 2 + lax.rem(z_lo + dz, 2))
        copy = send(n, dy, dz)
        copy.start()
        sent.append(copy)
        if n == 1:
            own_basis.wait()
            for copy in basis_copies:
                copy.wait()
            spread_far = remote(basis_rows(piece, 16), basis_rows(piece, 16), basis_send.at[7], basis_recv.at[7], far)
            spread_far.start()
        if n == 3:
            pass_along(2)
            spread_far.wait()
            two = piece - z_hi * 16
            spread_sides = [
                remote(basis_rows(two, 32), basis_rows(two, 32), basis_send.at[8 + k], basis_recv.at[8 + k], device)
                for k, device in enumerate(sides)
            ]
            for copy in spread_sides:
                copy.start()
        if n == 5:
            pass_along(1)
    own = pltpu.make_async_copy(chunk(gx), rows.at[gx], own_sem)
    own.start()
    own.wait()
    pass_along(3)

    def store(s):
        return pl.ds(pl.multiple_of(((s % 2) * 18 + s // 2) * BLOCK, BLOCK), BLOCK)

    def block(s):
        j = s % 8
        i = (j + s // 8) % 8
        left = jnp.concatenate([rows[j, z] for z in range(8)], axis=1)
        right = jnp.concatenate([rows[i, z] for z in range(8)], axis=1)
        partial[store(s), :] = lax.dot_general(left, right, (((1,), (1,)), ((), ())), preferred_element_type=F32)

        @pl.when(s % 2 != core)
        def _():
            swap(s // 2).start()

    def swap(n):
        src = partial.at[pl.ds(pl.multiple_of(((1 - core) * 18 + n) * BLOCK, BLOCK), BLOCK)]
        return remote(src, half_in.at[n], pair_send.at[n], pair_recv.at[n], sibling)

    def away(offset):
        return lax.rem(y + 4 - offset // 2, 4) * 2 + lax.rem(z_lo + offset, 2)

    arrivals = (0, 2, 6, 5, 4, 3, 7, 1)
    for n, offset in enumerate(arrivals):
        source = away(offset)
        if n > 0:
            there = rows.at[source]
            remote(there, there, send_sem.at[0], recv_sem.at[offset - 1], (source, gy, ft)).wait_recv()

        def pair(k, code):
            first = away(code % 8)
            d = (source + 8 - first) % 8
            far_side = d // 5
            half_way = d // 4 - far_side
            block(
                (1 - far_side - half_way) * (d * 8 + first)
                + far_side * ((8 - d) * 8 + source)
                + half_way * (32 + first % 4)
            )
            return code // 8

        lax.fori_loop(0, n + 1, pair, sum(o * 8**k for k, o in enumerate(arrivals)))
    for copy in spread_sides:
        copy.wait()
    eight = core * 128
    spread_pair = remote(basis_rows(eight, 128), basis_rows(eight, 128), basis_send.at[11], basis_recv.at[11], sibling)

    mine = pl.multiple_of(core * HALF, HALF)
    other = pl.multiple_of((1 - core) * HALF, HALF)

    def take(n, _):
        swap(n).wait()
        here = pl.ds(pl.multiple_of(mine + n * BLOCK, BLOCK), BLOCK)
        partial[here, :] = partial[here, :] + half_in[n]
        return 0

    lax.fori_loop(0, 18, take, 0)
    spread_pair.start()

    def add(first, count, sources, tile):
        def body(k, _):
            here = pl.ds(pl.multiple_of(first + k * tile, 8), tile)
            there = pl.ds(pl.multiple_of(k * tile, 8), tile)
            total = partial[here, :]
            for source in sources:
                total = total + source[there, :]
            partial[here, :] = total
            return 0

        lax.fori_loop(0, count // tile, body, 0)

    starts = [[mine + p * PART] for p in range(3)]
    sizes = [PART // 4, PART // 16, PART // 64]
    for depth, (inbox, send, recv) in enumerate(((in_1, send_1, recv_1), (in_2, send_2, recv_2), (in_3, send_3, recv_3))):
        size = sizes[depth]
        copies = []
        for o in (1, 3, 2):
            for p in range(3):
                t, device = peer((p + depth) % 3, o)
                src = pl.ds(pl.multiple_of(starts[p][depth] + t * size, 8), size)
                n = p * 3 + o - 1
                copies.append(remote(partial.at[src], inbox.at[n], send.at[n], recv.at[n], device))
        for copy in copies:
            copy.start()
        for copy in copies:
            copy.wait()
        for p in range(3):
            first = starts[p][depth] + coords[(p + depth) % 3] * size
            starts[p].append(first)
            add(first, size, [inbox.at[p * 3 + o] for o in range(3)], min(size, 96))

    for p in range(3):
        here = pl.ds(pl.multiple_of(starts[p][3], 8), sizes[2])
        gram[here, :] = partial[here, :]
    lasts = []

    def pass_on(p, first, n):
        here = gram.at[pl.ds(pl.multiple_of(first, 8), sizes[0])]
        copy = remote(here, here, last_send.at[n], last_recv.at[n], sibling)
        copy.start()
        lasts.append(copy)

    for depth, send, recv in ((2, back_3, home_3), (1, back_2, home_2), (0, back_1, home_1)):
        size = sizes[depth]
        copies = []
        for o in (1, 3, 2):
            for p in range(3):
                here = gram.at[pl.ds(pl.multiple_of(starts[p][depth + 1], 8), size)]
                _, device = peer((p + depth) % 3, o)
                n = p * 3 + o - 1
                copies.append(remote(here, here, send.at[n], recv.at[n], device))
        for copy in copies:
            copy.start()
        if depth == 0:
            for p in range(3):
                pass_on(p, starts[p][1], p * 4)
        for o in (1, 3, 2):
            for p in range(3):
                n = p * 3 + o - 1
                t, device = peer((p + depth) % 3, 4 - o)
                first = starts[p][depth] + t * size
                there = gram.at[pl.ds(pl.multiple_of(first, 8), size)]
                remote(there, there, send.at[n], recv.at[n], device).wait_recv()
                if depth == 0:
                    pass_on(p, first, p * 4 + o)
        for copy in copies:
            copy.wait_send()
    for p in range(3):
        for o in range(4):
            n = p * 4 + o
            t = lax.rem(coords[p] + 4 - o, 4)
            there = gram.at[pl.ds(pl.multiple_of(other + p * PART + t * sizes[0], 8), sizes[0])]
            remote(there, there, last_send.at[n], last_recv.at[n], sibling).wait_recv()
    for copy in lasts:
        copy.wait_send()
    spread_pair.wait()

    for copy in sent:
        copy.wait_send()


def step_and_gram(wind_field, terrain, start_basis):
    dma = pltpu.SemaphoreType.DMA
    return pl.pallas_call(
        gram_kernel,
        out_shape=(
            jax.ShapeDtypeStruct((4, 16, BLOCK, 128), BF16),
            jax.ShapeDtypeStruct((GX, 8, BLOCK, 128), BF16),
            jax.ShapeDtypeStruct((PAIRS * BLOCK, BLOCK), F32),
            jax.ShapeDtypeStruct((GX, BLOCK, BLOCK), F32),
        ),
        in_specs=[pl.BlockSpec(memory_space=VMEM)] * 3,
        out_specs=(pl.BlockSpec(memory_space=VMEM),) * 4,
        scratch_shapes=[
            VMEM((BLOCK, 128), BF16),
            VMEM((2, BLOCK, 128), BF16),
            VMEM((2, 64, 128), F32),
            VMEM((2, 64, 128), F32),
            VMEM((BLOCK, 128), F32),
            VMEM((BLOCK, BLOCK), BF16),
            VMEM((128, 128), BF16),
            VMEM((3, 8, BLOCK, 128), BF16),
            VMEM((PAIRS * BLOCK, BLOCK), F32),
            VMEM((18, BLOCK, BLOCK), F32),
            VMEM((9, PART // 4, BLOCK), F32),
            VMEM((9, PART // 16, BLOCK), F32),
            VMEM((9, PART // 64, BLOCK), F32),
            dma((4,)), dma((4,)), dma((7,)), dma((7,)), dma((3,)), dma((3,)), dma, dma((12,)), dma((12,)), dma,
            dma((18,)), dma((18,)),
        ]
        + [dma((9,))] * 12
        + [dma((12,))] * 2,
        compiler_params=pltpu.CompilerParams(collective_id=0, has_side_effects=True, vmem_limit_bytes=LIMIT),
        name="step_and_gram",
    )(wind_field, terrain, start_basis)


def core_kernel(basis_t, rows, core, stage, outbox, inbox, send_sem, recv_sem):
    gx, gy, ft = place()
    peers = [(lax.rem(gx + i, GX), gy, ft) for i in range(1, GX)]
    greet(peers)
    for z in range(0, 8, 2):
        total = jnp.zeros((BLOCK, BLOCK), F32)
        for j in range(GX):
            pair = jnp.concatenate([rows[j, z], rows[j, z + 1]], axis=1)
            total += jnp.dot(basis_t[:, j * BLOCK : (j + 1) * BLOCK], pair, preferred_element_type=F32)
        stage[:, z, :] = total[:, :128]
        stage[:, z + 1, :] = total[:, 128:]
    for r in range(GX):
        outbox[r] = stage[r * 32 : (r + 1) * 32].reshape(BLOCK, 128).astype(BF16)
    copies = []
    for i in range(1, GX):
        device = peers[i - 1]
        copies.append(remote(outbox.at[device[0]], inbox.at[gx], send_sem.at[i - 1], recv_sem.at[i - 1], device))
    for copy in copies:
        copy.start()
    inbox[gx] = outbox[gx]
    for i in range(1, GX):
        there = inbox.at[lax.rem(gx + GX - i, GX)]
        remote(there, there, send_sem.at[i - 1], recv_sem.at[i - 1], peers[GX - 1 - i]).wait_recv()
    for f in range(4):
        low = inbox[2 * f].astype(F32).reshape(32, 8, 128)
        high = inbox[2 * f + 1].astype(F32).reshape(32, 8, 128)
        core[:, f] = jnp.concatenate([low, high], axis=1).astype(BF16)
    for copy in copies:
        copy.wait_send()


def core_of(basis_t, rows):
    return pl.pallas_call(
        core_kernel,
        out_shape=jax.ShapeDtypeStruct((32, 4, 16, 128), BF16),
        in_specs=[pl.BlockSpec(memory_space=VMEM)] * 2,
        out_specs=pl.BlockSpec(memory_space=VMEM),
        scratch_shapes=[
            VMEM((BLOCK, 8, 128), F32),
            VMEM((GX, BLOCK, 128), BF16),
            VMEM((GX, BLOCK, 128), BF16),
            pltpu.SemaphoreType.DMA((7,)),
            pltpu.SemaphoreType.DMA((7,)),
        ],
        compiler_params=pltpu.CompilerParams(collective_id=1, has_side_effects=True, vmem_limit_bytes=LIMIT),
        name="core",
    )(basis_t, rows)


PANEL = 64
EXACT = lax.Precision.HIGHEST


def split(value):
    high = value.astype(BF16)
    return high, (value - high.astype(F32)).astype(BF16)


def eliminate(block):
    count = PANEL // 8
    line = lax.broadcasted_iota(jnp.int32, (8, 128), 0)
    lane = lax.broadcasted_iota(jnp.int32, (8, 128), 1)
    tiles = [jnp.where(lane == line + 8 * i, 1.0, block[8 * i : 8 * i + 8]) for i in range(count)]
    for g in range(count):
        first = PANEL + 8 * g
        spread = [[jnp.broadcast_to(tiles[i][:, first + t : first + t + 1], (8, 128)) for t in range(8)] for i in range(g, count)]
        scale = jnp.zeros((8, 128), F32)
        for t in range(8):
            pivot = jnp.broadcast_to(spread[0][t][t : t + 1], (8, 128))
            inverse = 1.0 / pivot
            scale = jnp.where(line == t, lax.rsqrt(pivot), scale)
            row = jnp.broadcast_to(tiles[g][t : t + 1], (8, 128))
            heads = [jnp.broadcast_to(spread[0][u][t : t + 1], (8, 128)) for u in range(t + 1, 8)]
            for n, i in enumerate(range(g, count)):
                factor = spread[n][t] * inverse
                if n == 0:
                    factor = jnp.where(line > t, factor, 0.0)
                tiles[i] = tiles[i] - factor * row
                for u in range(t + 1, 8):
                    spread[n][u] = spread[n][u] - factor * heads[u - t - 1]
        tiles[g] = tiles[g] * scale
    return jnp.concatenate(tiles, axis=0)


def invert_factor(work):
    for k in range(BLOCK // PANEL):
        here = slice(k * PANEL, (k + 1) * PANEL)
        base = (k // 2) * 128
        both = work[here, base : base + 128]
        if k % 2 == 0:
            both = pltpu.roll(both, PANEL, 1)
        lane = lax.broadcasted_iota(jnp.int32, both.shape, 1)
        small = eliminate(jnp.where(lane < PANEL, 0.0, both))[:, :PANEL]
        left, right = base, BLOCK + (k // 2 + 1) * 128
        rows = jnp.dot(small, work[here, left:right], precision=EXACT, preferred_element_type=F32)
        work[here, left:right] = rows
        if k + 1 < BLOCK // PANEL:
            below = (k + 1) * PANEL
            factor = rows[:, below - left : BLOCK - left]
            work[below:, left:right] = work[below:, left:right] - lax.dot_general(
                factor, rows, (((0,), (0,)), ((), ())), precision=EXACT, preferred_element_type=F32
            )


def iterate_kernel(blocks, start, basis, rounded, high_g, low_g, parts, image, current, work):
    gx = lax.axis_index("gx")

    def spread(n, _):
        s = (n % 18) * 2 + n // 18
        j = s % 8
        i = (j + s // 8) % 8
        block = blocks[pl.ds(pl.multiple_of(n * BLOCK, BLOCK), BLOCK), :]
        for row, column, value in ((j, i, block), (i, j, block.T)):
            high, low = split(value)
            high_g[column, pl.ds(pl.multiple_of(row * BLOCK, BLOCK), BLOCK), :] = high
            low_g[column, pl.ds(pl.multiple_of(row * BLOCK, BLOCK), BLOCK), :] = low
        return 0

    lax.fori_loop(0, PAIRS, spread, 0)

    def columns(j):
        return pl.ds(pl.multiple_of(j * BLOCK, BLOCK), BLOCK)

    def keep(j, value):
        high, low = split(value)
        parts[0:BLOCK, columns(j)] = high
        parts[BLOCK:, columns(j)] = low

    def load(j, _):
        keep(j, start[j].T)
        return 0

    lax.fori_loop(0, GX, load, 0)
    unit = jnp.where(
        lax.broadcasted_iota(jnp.int32, (BLOCK, BLOCK), 0) == lax.broadcasted_iota(jnp.int32, (BLOCK, BLOCK), 1), 1.0, 0.0
    )

    def iteration(_, carry):
        work[:, 0:BLOCK] = jnp.zeros((BLOCK, BLOCK), F32)
        work[:, BLOCK:] = jnp.zeros((BLOCK, BLOCK), F32)

        def multiply(j, _):
            both = jnp.dot(parts[...], high_g[j], preferred_element_type=F32)
            value = both[:BLOCK] + (both[BLOCK:] + jnp.dot(parts[0:BLOCK, :], low_g[j], preferred_element_type=F32))
            high, middle = split(value)
            low = (value - high.astype(F32) - middle.astype(F32)).astype(BF16)
            image[0:BLOCK, columns(j)] = high
            image[BLOCK:, columns(j)] = middle
            across = (((1,), (1,)), ((), ()))
            three = lax.dot_general(
                jnp.concatenate([high, middle, low], axis=0), high, across, preferred_element_type=F32
            )
            work[:, 0:BLOCK] += three[:BLOCK] + lax.dot_general(middle, middle, across, preferred_element_type=F32)
            work[:, BLOCK:] += three[BLOCK : 2 * BLOCK] + three[2 * BLOCK :]
            return 0

        lax.fori_loop(0, GX, multiply, 0)
        mixed = work[:, BLOCK:]
        work[:, 0:BLOCK] += mixed + mixed.T
        work[:, BLOCK:] = unit
        invert_factor(work)
        high, low = split(work[:, BLOCK:])
        factor = jnp.concatenate([high, low], axis=0)

        def apply(j, _):
            both = jnp.dot(factor, image[0:BLOCK, columns(j)], preferred_element_type=F32)
            value = both[:BLOCK] + (
                both[BLOCK:] + jnp.dot(factor[:BLOCK], image[BLOCK:, columns(j)], preferred_element_type=F32)
            )
            current[:, columns(j)] = value
            keep(j, value)
            return 0

        lax.fori_loop(0, GX, apply, 0)
        return carry

    lax.fori_loop(0, ITERS, iteration, 0)
    basis[...] = current[:, columns(gx)].T
    rounded[...] = parts[0:BLOCK, :]


def iterate(blocks, start):
    return pl.pallas_call(
        iterate_kernel,
        out_shape=(jax.ShapeDtypeStruct((BLOCK, BLOCK), F32), jax.ShapeDtypeStruct((BLOCK, GX * BLOCK), BF16)),
        in_specs=[pl.BlockSpec(memory_space=VMEM)] * 2,
        out_specs=(pl.BlockSpec(memory_space=VMEM),) * 2,
        scratch_shapes=[
            VMEM((GX, GX * BLOCK, BLOCK), BF16),
            VMEM((GX, GX * BLOCK, BLOCK), BF16),
            VMEM((2 * BLOCK, GX * BLOCK), BF16),
            VMEM((2 * BLOCK, GX * BLOCK), BF16),
            VMEM((BLOCK, GX * BLOCK), F32),
            VMEM((BLOCK, 2 * BLOCK), F32),
        ],
        compiler_params=pltpu.CompilerParams(vmem_limit_bytes=LIMIT),
        name="iterate",
    )(blocks, start)


def per_device(wind_field, terrain, start_basis):
    advanced, rows, blocks, basis = step_and_gram(wind_field, terrain, start_basis)
    basis_rows, rounded = iterate(blocks, basis)
    core = core_of(rounded, rows)
    return (advanced, basis_rows, core)


def solution(mesh):
    placed = (P("ft", None, "gx", "gy"), P("gx", "gy"), P("gx", None))
    return jax.shard_map(
        per_device,
        mesh=mesh,
        in_specs=placed,
        out_specs=(P("ft", None, "gx", "gy"), P("gx", None), P("gx", "ft", None, "gy")),
        check_vma=False,
    )
```

```python
import functools

import jax
import jax.numpy as jnp
from jax import lax
from jax.experimental import pallas as pl
from jax.experimental.pallas import tpu as pltpu
from jax.sharding import PartitionSpec as P

ITERS = 4
MESH = pl.DeviceIdType.MESH
VMEM = pltpu.VMEM
F32 = jnp.float32
BF16 = jnp.bfloat16
GX = 8
BLOCK = 256
PAIRS = 36
LIMIT = 56 * 1024 * 1024

diffusion_number = 0.15


def place():
    return lax.axis_index("gx"), lax.axis_index("gy"), lax.axis_index("ft")


def greet(devices):
    barrier = pltpu.get_barrier_semaphore()
    for device in devices:
        pl.semaphore_signal(barrier, inc=1, device_id=device, device_id_type=MESH)
    pl.semaphore_wait(barrier, len(devices))


def remote(src, dst, send, recv, device):
    return pltpu.make_async_remote_copy(
        src_ref=src, dst_ref=dst, send_sem=send, recv_sem=recv, device_id=device, device_id_type=MESH
    )


HALF = 18 * BLOCK
PART = HALF // 3


def gram_kernel(
    wind, terrain, start, advanced, rows, gram, basis,
    edge_out, edge_in, line_out, line_in, merged, near_x, near_y,
    relay, partial, half_in, in_1, in_2, in_3,
    halo_send, halo_recv, send_sem, recv_sem, relay_send, relay_recv, own_sem, basis_send, basis_recv, basis_own,
    pair_send, pair_recv, send_1, recv_1, send_2, recv_2, send_3, recv_3,
    back_3, home_3, back_2, home_2, back_1, home_1, last_send, last_recv,
):
    gx, gy, ft = place()
    core, z_hi = ft % 2, ft // 2
    coords = (gy, gx // 2, z_hi * 2 + gx % 2)

    def at(axis, t):
        if axis == 0:
            return (gx, t, ft)
        if axis == 1:
            return (t * 2 + gx % 2, gy, ft)
        return ((gx // 2) * 2 + t % 2, gy, (t // 2) * 2 + core)

    def peer(axis, o):
        t = lax.rem(coords[axis] + o, 4)
        return t, at(axis, t)

    y, z_lo = gx // 2, gx % 2
    beside = (y * 2 + 1 - z_lo, gy, ft)
    peers = [(lax.rem(gx + i, GX), gy, ft) for i in range(1, GX)]
    sides = [(gx, lax.rem(gy + o, 4), ft) for o in range(1, 4)]
    sibling = (gx, gy, z_hi * 2 + 1 - core)
    far = (gx, gy, lax.rem(ft + 2, 4))
    far_odd = ((gx // 2) * 2 + 1 - gx % 2, gy, lax.rem(ft + 2, 4))
    greet(peers + sides + [sibling, far, far_odd])

    def basis_rows(first, count):
        return basis.at[:, pl.ds(pl.multiple_of(first, 16), count)]

    piece = (core * 8 + gy * 2 + z_hi) * 16
    here = pl.ds(pl.multiple_of(piece, 16), 16)
    basis_copies = [
        remote(start.at[here], basis.at[gx, here], basis_send.at[n], basis_recv.at[n], device) for n, device in enumerate(peers)
    ]
    for copy in basis_copies:
        copy.start()
    own_basis = pltpu.make_async_copy(start.at[here], basis.at[gx, here], basis_own)
    own_basis.start()

    lane = lax.broadcasted_iota(jnp.int32, (BLOCK, 128), 1)
    line = lax.broadcasted_iota(jnp.int32, (BLOCK, 128), 0)

    def collect(k, packed):
        tile = wind[k // 16, k % 16].astype(F32)
        line_out[0, pl.ds(k, 1), :] = tile[0:1]
        line_out[1, pl.ds(k, 1), :] = tile[BLOCK - 1 : BLOCK]
        return jnp.where(lane // 2 == k, pltpu.roll(tile, 2 * k + 1, 1), packed)

    packed = lax.fori_loop(0, 64, collect, jnp.zeros((BLOCK, 128), F32))
    edge_out[...] = packed.astype(BF16)
    halos = [
        remote(line_out.at[1], line_in.at[0], halo_send.at[0], halo_recv.at[0], peers[0]),
        remote(line_out.at[0], line_in.at[1], halo_send.at[1], halo_recv.at[1], peers[6]),
        remote(edge_out, edge_in.at[0], halo_send.at[2], halo_recv.at[2], sides[0]),
        remote(edge_out, edge_in.at[1], halo_send.at[3], halo_recv.at[3], sides[2]),
    ]
    for copy in halos:
        copy.start()
    a = lax.broadcasted_iota(jnp.int32, (BLOCK, BLOCK), 0)
    b = lax.broadcasted_iota(jnp.int32, (BLOCK, BLOCK), 1)
    near_x[...] = jnp.where(jnp.abs(a - b) == 1, 1.0, 0.0).astype(BF16)
    near_y[...] = near_x[0:128, 0:128]
    for copy in halos:
        copy.wait()
    from_before = pltpu.roll(edge_in[0].astype(F32), 1, 1)
    from_after = pltpu.roll(edge_in[1].astype(F32), 127, 1)
    merged[...] = jnp.where(lane % 2 == 0, from_after, from_before)

    def chunk(c):
        field, first = c // 2, (c % 2) * 8

        def level(i, _):
            z = first + i
            k = field * 16 + z
            tile = wind[field, z]
            center = tile.astype(F32)
            above = wind[field, lax.rem(z + 1, 16)].astype(F32)
            below = wind[field, lax.rem(z + 15, 16)].astype(F32)
            around = jnp.where(z < 15, above, 0.0) + jnp.where(z > 0, below, 0.0)
            around += jnp.dot(near_x[...], tile, preferred_element_type=F32)
            around += jnp.dot(tile, near_y[...], preferred_element_type=F32)
            side = pltpu.roll(merged[...], 127 - 2 * k, 1)
            around += jnp.where((lane == 0) | (lane == 127), side, 0.0)
            around += jnp.where(line == 0, line_in[0, pl.ds(k, 1), :], 0.0)
            around += jnp.where(line == BLOCK - 1, line_in[1, pl.ds(k, 1), :], 0.0)
            stepped = center + diffusion_number * (around - 6.0 * center)
            advanced[field, z] = jnp.where(z >= terrain[...], stepped, 0.0).astype(BF16)
            return 0

        lax.fori_loop(0, 8, level, 0)
        return advanced.at[field, pl.ds(first, 8)]

    def send(n, dy, dz):
        c = lax.rem(y + dy, 4) * 2 + lax.rem(z_lo + dz, 2)
        part = advanced.at[c // 2, pl.ds((c % 2) * 8, 8)]
        if dz == 1 and dy > 0:
            return remote(part, relay.at[dy - 1], send_sem.at[n], relay_recv.at[dy - 1], beside)
        return remote(part, rows.at[gx], send_sem.at[n], recv_sem.at[dy * 2 + dz - 1], (c, gy, ft))

    def pass_along(dy):
        arrived = relay.at[dy - 1]
        remote(arrived, arrived, relay_send.at[dy - 1], relay_recv.at[dy - 1], beside).wait_recv()
        target = (lax.rem(y + dy, 4) * 2 + z_lo, gy, ft)
        copy = remote(arrived, rows.at[beside[0]], relay_send.at[dy - 1], recv_sem.at[dy * 2], target)
        copy.start()
        sent.append(copy)

    sent = []
    for n, (dy, dz) in enumerate(((2, 1), (1, 0), (1, 1), (3, 0), (3, 1), (2, 0), (0, 1))):
        chunk(lax.rem(y + dy, 4) * 2 + lax.rem(z_lo + dz, 2))
        copy = send(n, dy, dz)
        copy.start()
        sent.append(copy)
        if n == 1:
            own_basis.wait()
            for copy in basis_copies:
                copy.wait()
            spread_far = remote(basis_rows(piece, 16), basis_rows(piece, 16), basis_send.at[7], basis_recv.at[7], far)
            spread_far.start()
        if n == 3:
            pass_along(2)
            spread_far.wait()
            two = piece - z_hi * 16
            spread_sides = [
                remote(basis_rows(two, 32), basis_rows(two, 32), basis_send.at[8 + k], basis_recv.at[8 + k], device)
                for k, device in enumerate(sides)
            ]
            for copy in spread_sides:
                copy.start()
        if n == 5:
            pass_along(1)
    own = pltpu.make_async_copy(chunk(gx), rows.at[gx], own_sem)
    own.start()
    own.wait()
    pass_along(3)

    def store(s):
        return pl.ds(pl.multiple_of(((s % 2) * 18 + s // 2) * BLOCK, BLOCK), BLOCK)

    def block(s):
        j = s % 8
        i = (j + s // 8) % 8
        left = jnp.concatenate([rows[j, z] for z in range(8)], axis=1)
        right = jnp.concatenate([rows[i, z] for z in range(8)], axis=1)
        partial[store(s), :] = lax.dot_general(left, right, (((1,), (1,)), ((), ())), preferred_element_type=F32)

        @pl.when(s % 2 != core)
        def _():
            swap(s // 2).start()

    def swap(n):
        src = partial.at[pl.ds(pl.multiple_of(((1 - core) * 18 + n) * BLOCK, BLOCK), BLOCK)]
        return remote(src, half_in.at[n], pair_send.at[n], pair_recv.at[n], sibling)

    def away(offset):
        return lax.rem(y + 4 - offset // 2, 4) * 2 + lax.rem(z_lo + offset, 2)

    arrivals = (0, 2, 6, 5, 4, 3, 7, 1)
    for n, offset in enumerate(arrivals):
        source = away(offset)
        if n > 0:
            there = rows.at[source]
            remote(there, there, send_sem.at[0], recv_sem.at[offset - 1], (source, gy, ft)).wait_recv()

        def pair(k, code):
            first = away(code % 8)
            d = (source + 8 - first) % 8
            far_side = d // 5
            half_way = d // 4 - far_side
            block(
                (1 - far_side - half_way) * (d * 8 + first)
                + far_side * ((8 - d) * 8 + source)
                + half_way * (32 + first % 4)
            )
            return code // 8

        lax.fori_loop(0, n + 1, pair, sum(o * 8**k for k, o in enumerate(arrivals)))
    for copy in spread_sides:
        copy.wait()
    eight = core * 128
    spread_pair = remote(basis_rows(eight, 128), basis_rows(eight, 128), basis_send.at[11], basis_recv.at[11], sibling)

    mine = pl.multiple_of(core * HALF, HALF)
    other = pl.multiple_of((1 - core) * HALF, HALF)

    def take(n, _):
        swap(n).wait()
        here = pl.ds(pl.multiple_of(mine + n * BLOCK, BLOCK), BLOCK)
        partial[here, :] = partial[here, :] + half_in[n]
        return 0

    lax.fori_loop(0, 18, take, 0)
    spread_pair.start()

    def add(first, count, sources, tile):
        def body(k, _):
            here = pl.ds(pl.multiple_of(first + k * tile, 8), tile)
            there = pl.ds(pl.multiple_of(k * tile, 8), tile)
            total = partial[here, :]
            for source in sources:
                total = total + source[there, :]
            partial[here, :] = total
            return 0

        lax.fori_loop(0, count // tile, body, 0)

    starts = [[mine + p * PART] for p in range(3)]
    sizes = [PART // 4, PART // 16, PART // 64]
    for depth, (inbox, send, recv) in enumerate(((in_1, send_1, recv_1), (in_2, send_2, recv_2), (in_3, send_3, recv_3))):
        size = sizes[depth]
        copies = []
        for o in (1, 3, 2):
            for p in range(3):
                t, device = peer((p + depth) % 3, o)
                src = pl.ds(pl.multiple_of(starts[p][depth] + t * size, 8), size)
                n = p * 3 + o - 1
                copies.append(remote(partial.at[src], inbox.at[n], send.at[n], recv.at[n], device))
        for copy in copies:
            copy.start()
        for copy in copies:
            copy.wait()
        for p in range(3):
            first = starts[p][depth] + coords[(p + depth) % 3] * size
            starts[p].append(first)
            add(first, size, [inbox.at[p * 3 + o] for o in range(3)], min(size, 96))

    for p in range(3):
        here = pl.ds(pl.multiple_of(starts[p][3], 8), sizes[2])
        gram[here, :] = partial[here, :]
    lasts = []

    def pass_on(p, first, n):
        here = gram.at[pl.ds(pl.multiple_of(first, 8), sizes[0])]
        copy = remote(here, here, last_send.at[n], last_recv.at[n], sibling)
        copy.start()
        lasts.append(copy)

    for depth, send, recv in ((2, back_3, home_3), (1, back_2, home_2), (0, back_1, home_1)):
        size = sizes[depth]
        copies = []
        for o in (1, 3, 2):
            for p in range(3):
                here = gram.at[pl.ds(pl.multiple_of(starts[p][depth + 1], 8), size)]
                _, device = peer((p + depth) % 3, o)
                n = p * 3 + o - 1
                copies.append(remote(here, here, send.at[n], recv.at[n], device))
        for copy in copies:
            copy.start()
        if depth == 0:
            for p in range(3):
                pass_on(p, starts[p][1], p * 4)
        for o in (1, 3, 2):
            for p in range(3):
                n = p * 3 + o - 1
                t, device = peer((p + depth) % 3, 4 - o)
                first = starts[p][depth] + t * size
                there = gram.at[pl.ds(pl.multiple_of(first, 8), size)]
                remote(there, there, send.at[n], recv.at[n], device).wait_recv()
                if depth == 0:
                    pass_on(p, first, p * 4 + o)
        for copy in copies:
            copy.wait_send()
    for p in range(3):
        for o in range(4):
            n = p * 4 + o
            t = lax.rem(coords[p] + 4 - o, 4)
            there = gram.at[pl.ds(pl.multiple_of(other + p * PART + t * sizes[0], 8), sizes[0])]
            remote(there, there, last_send.at[n], last_recv.at[n], sibling).wait_recv()
    for copy in lasts:
        copy.wait_send()
    spread_pair.wait()

    for copy in sent:
        copy.wait_send()


def step_and_gram(wind_field, terrain, start_basis):
    dma = pltpu.SemaphoreType.DMA
    return pl.pallas_call(
        gram_kernel,
        out_shape=(
            jax.ShapeDtypeStruct((4, 16, BLOCK, 128), BF16),
            jax.ShapeDtypeStruct((GX, 8, BLOCK, 128), BF16),
            jax.ShapeDtypeStruct((PAIRS * BLOCK, BLOCK), F32),
            jax.ShapeDtypeStruct((GX, BLOCK, BLOCK), F32),
        ),
        in_specs=[pl.BlockSpec(memory_space=VMEM)] * 3,
        out_specs=(pl.BlockSpec(memory_space=VMEM),) * 4,
        scratch_shapes=[
            VMEM((BLOCK, 128), BF16),
            VMEM((2, BLOCK, 128), BF16),
            VMEM((2, 64, 128), F32),
            VMEM((2, 64, 128), F32),
            VMEM((BLOCK, 128), F32),
            VMEM((BLOCK, BLOCK), BF16),
            VMEM((128, 128), BF16),
            VMEM((3, 8, BLOCK, 128), BF16),
            VMEM((PAIRS * BLOCK, BLOCK), F32),
            VMEM((18, BLOCK, BLOCK), F32),
            VMEM((9, PART // 4, BLOCK), F32),
            VMEM((9, PART // 16, BLOCK), F32),
            VMEM((9, PART // 64, BLOCK), F32),
            dma((4,)), dma((4,)), dma((7,)), dma((7,)), dma((3,)), dma((3,)), dma, dma((12,)), dma((12,)), dma,
            dma((18,)), dma((18,)),
        ]
        + [dma((9,))] * 12
        + [dma((12,))] * 2,
        compiler_params=pltpu.CompilerParams(collective_id=0, has_side_effects=True, vmem_limit_bytes=LIMIT),
        name="step_and_gram",
    )(wind_field, terrain, start_basis)


def core_kernel(basis_t, rows, core, stage, outbox, inbox, send_sem, recv_sem):
    gx, gy, ft = place()
    peers = [(lax.rem(gx + i, GX), gy, ft) for i in range(1, GX)]
    greet(peers)
    for z in range(0, 8, 2):
        total = jnp.zeros((BLOCK, BLOCK), F32)
        for j in range(GX):
            pair = jnp.concatenate([rows[j, z], rows[j, z + 1]], axis=1)
            total += jnp.dot(basis_t[:, j * BLOCK : (j + 1) * BLOCK], pair, preferred_element_type=F32)
        stage[:, z, :] = total[:, :128]
        stage[:, z + 1, :] = total[:, 128:]
    for r in range(GX):
        outbox[r] = stage[r * 32 : (r + 1) * 32].reshape(BLOCK, 128).astype(BF16)
    copies = []
    for i in range(1, GX):
        device = peers[i - 1]
        copies.append(remote(outbox.at[device[0]], inbox.at[gx], send_sem.at[i - 1], recv_sem.at[i - 1], device))
    for copy in copies:
        copy.start()
    inbox[gx] = outbox[gx]
    for i in range(1, GX):
        there = inbox.at[lax.rem(gx + GX - i, GX)]
        remote(there, there, send_sem.at[i - 1], recv_sem.at[i - 1], peers[GX - 1 - i]).wait_recv()
    for f in range(4):
        low = inbox[2 * f].astype(F32).reshape(32, 8, 128)
        high = inbox[2 * f + 1].astype(F32).reshape(32, 8, 128)
        core[:, f] = jnp.concatenate([low, high], axis=1).astype(BF16)
    for copy in copies:
        copy.wait_send()


def core_of(basis_t, rows):
    return pl.pallas_call(
        core_kernel,
        out_shape=jax.ShapeDtypeStruct((32, 4, 16, 128), BF16),
        in_specs=[pl.BlockSpec(memory_space=VMEM)] * 2,
        out_specs=pl.BlockSpec(memory_space=VMEM),
        scratch_shapes=[
            VMEM((BLOCK, 8, 128), F32),
            VMEM((GX, BLOCK, 128), BF16),
            VMEM((GX, BLOCK, 128), BF16),
            pltpu.SemaphoreType.DMA((7,)),
            pltpu.SemaphoreType.DMA((7,)),
        ],
        compiler_params=pltpu.CompilerParams(collective_id=1, has_side_effects=True, vmem_limit_bytes=LIMIT),
        name="core",
    )(basis_t, rows)


PANEL = 64
EXACT = lax.Precision.HIGHEST


def split(value):
    high = value.astype(BF16)
    return high, (value - high.astype(F32)).astype(BF16)


def eliminate(block):
    count = PANEL // 8
    line = lax.broadcasted_iota(jnp.int32, (8, 128), 0)
    lane = lax.broadcasted_iota(jnp.int32, (8, 128), 1)
    tiles = [jnp.where(lane == line + 8 * i, 1.0, block[8 * i : 8 * i + 8]) for i in range(count)]
    for g in range(count):
        first = PANEL + 8 * g
        spread = [[jnp.broadcast_to(tiles[i][:, first + t : first + t + 1], (8, 128)) for t in range(8)] for i in range(g, count)]
        scale = jnp.zeros((8, 128), F32)
        for t in range(8):
            pivot = jnp.broadcast_to(spread[0][t][t : t + 1], (8, 128))
            inverse = 1.0 / pivot
            scale = jnp.where(line == t, lax.rsqrt(pivot), scale)
            row = jnp.broadcast_to(tiles[g][t : t + 1], (8, 128))
            heads = [jnp.broadcast_to(spread[0][u][t : t + 1], (8, 128)) for u in range(t + 1, 8)]
            for n, i in enumerate(range(g, count)):
                factor = spread[n][t] * inverse
                if n == 0:
                    factor = jnp.where(line > t, factor, 0.0)
                tiles[i] = tiles[i] - factor * row
                for u in range(t + 1, 8):
                    spread[n][u] = spread[n][u] - factor * heads[u - t - 1]
        tiles[g] = tiles[g] * scale
    return jnp.concatenate(tiles, axis=0)


def invert_factor(work, beside=lambda k: None):
    for k in range(BLOCK // PANEL):
        here = slice(k * PANEL, (k + 1) * PANEL)
        base = (k // 2) * 128
        both = work[here, base : base + 128]
        if k % 2 == 0:
            both = pltpu.roll(both, PANEL, 1)
        lane = lax.broadcasted_iota(jnp.int32, both.shape, 1)
        beside(2 * k)
        small = eliminate(jnp.where(lane < PANEL, 0.0, both))[:, :PANEL]
        beside(2 * k + 1)
        left, right = base, BLOCK + (k // 2 + 1) * 128
        rows = jnp.dot(small, work[here, left:right], precision=EXACT, preferred_element_type=F32)
        work[here, left:right] = rows
        if k + 1 < BLOCK // PANEL:
            below = (k + 1) * PANEL
            factor = rows[:, below - left : BLOCK - left]
            work[below:, left:right] = work[below:, left:right] - lax.dot_general(
                factor, rows, (((0,), (0,)), ((), ())), precision=EXACT, preferred_element_type=F32
            )


def iterate_kernel(blocks, start, basis, rounded, high_g, low_g, parts, image, current, work):
    gx = lax.axis_index("gx")

    def spread(n, _):
        s = (n % 18) * 2 + n // 18
        j = s % 8
        i = (j + s // 8) % 8
        block = blocks[pl.ds(pl.multiple_of(n * BLOCK, BLOCK), BLOCK), :]
        for row, column, value in ((j, i, block), (i, j, block.T)):
            high, low = split(value)
            high_g[column, pl.ds(pl.multiple_of(row * BLOCK, BLOCK), BLOCK), :] = high
            low_g[column, pl.ds(pl.multiple_of(row * BLOCK, BLOCK), BLOCK), :] = low
        return 0

    lax.fori_loop(0, PAIRS, spread, 0, unroll=2)

    def columns(j):
        return pl.ds(pl.multiple_of(j * BLOCK, BLOCK), BLOCK)

    def keep(j, value):
        high, low = split(value)
        parts[0:BLOCK, columns(j)] = high
        parts[BLOCK:, columns(j)] = low

    def load(j, _):
        keep(j, start[j].T)
        return 0

    lax.fori_loop(0, GX, load, 0)
    unit = jnp.where(
        lax.broadcasted_iota(jnp.int32, (BLOCK, BLOCK), 0) == lax.broadcasted_iota(jnp.int32, (BLOCK, BLOCK), 1), 1.0, 0.0
    )

    across = (((1,), (1,)), ((), ()))

    def times_gram(source, j):
        both = jnp.dot(source[...], high_g[j], preferred_element_type=F32)
        return both[:BLOCK] + (both[BLOCK:] + jnp.dot(source[0:BLOCK, :], low_g[j], preferred_element_type=F32))

    def clear():
        work[...] = jnp.zeros((BLOCK, 2 * BLOCK), F32)

    def add_products(j, value):
        high, middle = split(value)
        low = (value - high.astype(F32) - middle.astype(F32)).astype(BF16)
        image[0:BLOCK, columns(j)] = high
        image[BLOCK:, columns(j)] = middle
        three = lax.dot_general(jnp.concatenate([high, middle, low], axis=0), high, across, preferred_element_type=F32)
        work[:, 0:BLOCK] += three[:BLOCK] + lax.dot_general(middle, middle, across, preferred_element_type=F32)
        work[:, BLOCK:] += three[BLOCK : 2 * BLOCK] + three[2 * BLOCK :]

    def inverse_factor(beside):
        mixed = work[:, BLOCK:]
        work[:, 0:BLOCK] += mixed + mixed.T
        work[:, BLOCK:] = unit
        invert_factor(work, beside)
        high, low = split(work[:, BLOCK:])
        return jnp.concatenate([high, low], axis=0)

    def times_factor(factor, source, j):
        both = jnp.dot(factor, source[0:BLOCK, columns(j)], preferred_element_type=F32)
        return both[:BLOCK] + (
            both[BLOCK:] + jnp.dot(factor[:BLOCK], source[BLOCK:, columns(j)], preferred_element_type=F32)
        )

    def first(j, _):
        add_products(j, times_gram(parts, j))
        return 0

    clear()
    lax.fori_loop(0, GX, first, 0, unroll=2)

    def beside(j):
        keep(j, times_gram(image, j))

    def iteration(_, carry):
        factor = inverse_factor(beside)
        clear()

        def apply(j, _):
            add_products(j, times_factor(factor, parts, j))
            return 0

        lax.fori_loop(0, GX, apply, 0, unroll=4)
        return carry

    lax.fori_loop(0, ITERS - 1, iteration, 0)
    factor = inverse_factor(lambda j: None)

    def last(j, _):
        value = times_factor(factor, image, j)
        current[:, columns(j)] = value
        parts[0:BLOCK, columns(j)] = value.astype(BF16)
        return 0

    lax.fori_loop(0, GX, last, 0, unroll=4)
    basis[...] = current[:, columns(gx)].T
    rounded[...] = parts[0:BLOCK, :]


def iterate(blocks, start):
    return pl.pallas_call(
        iterate_kernel,
        out_shape=(jax.ShapeDtypeStruct((BLOCK, BLOCK), F32), jax.ShapeDtypeStruct((BLOCK, GX * BLOCK), BF16)),
        in_specs=[pl.BlockSpec(memory_space=VMEM)] * 2,
        out_specs=(pl.BlockSpec(memory_space=VMEM),) * 2,
        scratch_shapes=[
            VMEM((GX, GX * BLOCK, BLOCK), BF16),
            VMEM((GX, GX * BLOCK, BLOCK), BF16),
            VMEM((2 * BLOCK, GX * BLOCK), BF16),
            VMEM((2 * BLOCK, GX * BLOCK), BF16),
            VMEM((BLOCK, GX * BLOCK), F32),
            VMEM((BLOCK, 2 * BLOCK), F32),
        ],
        compiler_params=pltpu.CompilerParams(vmem_limit_bytes=LIMIT),
        name="iterate",
    )(blocks, start)


def per_device(wind_field, terrain, start_basis):
    advanced, rows, blocks, basis = step_and_gram(wind_field, terrain, start_basis)
    basis_rows, rounded = iterate(blocks, basis)
    core = core_of(rounded, rows)
    return (advanced, basis_rows, core)


def solution(mesh):
    placed = (P("ft", None, "gx", "gy"), P("gx", "gy"), P("gx", None))
    return jax.shard_map(
        per_device,
        mesh=mesh,
        in_specs=placed,
        out_specs=(P("ft", None, "gx", "gy"), P("gx", None), P("gx", "ft", None, "gy")),
        check_vma=False,
    )
```

```python
import functools

import jax
import jax.numpy as jnp
from jax import lax
from jax.experimental import pallas as pl
from jax.experimental.pallas import tpu as pltpu
from jax.sharding import PartitionSpec as P

ITERS = 4
MESH = pl.DeviceIdType.MESH
VMEM = pltpu.VMEM
F32 = jnp.float32
BF16 = jnp.bfloat16
GX = 8
BLOCK = 256
PAIRS = 36
LIMIT = 56 * 1024 * 1024

diffusion_number = 0.15


def place():
    return lax.axis_index("gx"), lax.axis_index("gy"), lax.axis_index("ft")


def greet(devices):
    barrier = pltpu.get_barrier_semaphore()
    for device in devices:
        pl.semaphore_signal(barrier, inc=1, device_id=device, device_id_type=MESH)
    return lambda: pl.semaphore_wait(barrier, len(devices))


def remote(src, dst, send, recv, device):
    return pltpu.make_async_remote_copy(
        src_ref=src, dst_ref=dst, send_sem=send, recv_sem=recv, device_id=device, device_id_type=MESH
    )


HALF = 18 * BLOCK
PART = HALF // 3


def gram_kernel(
    wind, terrain, start, advanced_out, rows_out, gram_out, basis_out,
    advanced, rows, gram, basis, out_sem, gram_sem,
    edge_out, edge_in, line_out, line_in, merged, near_x, near_y,
    relay, partial, half_in, in_1, in_2, in_3,
    halo_send, halo_recv, send_sem, recv_sem, relay_send, relay_recv, own_sem, basis_send, basis_recv, basis_own,
    pair_send, pair_recv, send_1, recv_1, send_2, recv_2, send_3, recv_3,
    back_3, home_3, back_2, home_2, back_1, home_1, last_send, last_recv,
):
    gx, gy, ft = place()
    core, z_hi = ft % 2, ft // 2
    coords = (gy, gx // 2, z_hi * 2 + gx % 2)

    def at(axis, t):
        if axis == 0:
            return (gx, t, ft)
        if axis == 1:
            return (t * 2 + gx % 2, gy, ft)
        return ((gx // 2) * 2 + t % 2, gy, (t // 2) * 2 + core)

    def peer(axis, o):
        t = lax.rem(coords[axis] + o, 4)
        return t, at(axis, t)

    y, z_lo = gx // 2, gx % 2
    beside = (y * 2 + 1 - z_lo, gy, ft)
    peers = [(lax.rem(gx + i, GX), gy, ft) for i in range(1, GX)]
    sides = [(gx, lax.rem(gy + o, 4), ft) for o in range(1, 4)]
    sibling = (gx, gy, z_hi * 2 + 1 - core)
    far = (gx, gy, lax.rem(ft + 2, 4))
    far_odd = ((gx // 2) * 2 + 1 - gx % 2, gy, lax.rem(ft + 2, 4))
    all_here = greet(peers + sides + [sibling, far, far_odd])

    def basis_rows(first, count):
        return basis.at[:, pl.ds(pl.multiple_of(first, 16), count)]

    piece = (core * 8 + gy * 2 + z_hi) * 16
    here = pl.ds(pl.multiple_of(piece, 16), 16)
    lane = lax.broadcasted_iota(jnp.int32, (BLOCK, 128), 1)
    line = lax.broadcasted_iota(jnp.int32, (BLOCK, 128), 0)

    def collect(k, packed):
        tile = wind[k // 16, k % 16].astype(F32)
        line_out[0, pl.ds(k, 1), :] = tile[0:1]
        line_out[1, pl.ds(k, 1), :] = tile[BLOCK - 1 : BLOCK]
        return jnp.where(lane // 2 == k, pltpu.roll(tile, 2 * k + 1, 1), packed)

    packed = lax.fori_loop(0, 64, collect, jnp.zeros((BLOCK, 128), F32), unroll=2)
    edge_out[...] = packed.astype(BF16)
    halos = [
        remote(line_out.at[1], line_in.at[0], halo_send.at[0], halo_recv.at[0], peers[0]),
        remote(line_out.at[0], line_in.at[1], halo_send.at[1], halo_recv.at[1], peers[6]),
        remote(edge_out, edge_in.at[0], halo_send.at[2], halo_recv.at[2], sides[0]),
        remote(edge_out, edge_in.at[1], halo_send.at[3], halo_recv.at[3], sides[2]),
    ]
    all_here()
    for copy in halos:
        copy.start()
    basis_copies = [
        remote(start.at[here], basis.at[gx, here], basis_send.at[n], basis_recv.at[n], device) for n, device in enumerate(peers)
    ]
    for copy in basis_copies:
        copy.start()
    own_basis = pltpu.make_async_copy(start.at[here], basis.at[gx, here], basis_own)
    own_basis.start()
    a = lax.broadcasted_iota(jnp.int32, (BLOCK, BLOCK), 0)
    b = lax.broadcasted_iota(jnp.int32, (BLOCK, BLOCK), 1)
    near_x[...] = jnp.where(jnp.abs(a - b) == 1, 1.0, 0.0).astype(BF16)
    near_y[...] = near_x[0:128, 0:128]
    for copy in halos:
        copy.wait()
    from_before = pltpu.roll(edge_in[0].astype(F32), 1, 1)
    from_after = pltpu.roll(edge_in[1].astype(F32), 127, 1)
    merged[...] = jnp.where(lane % 2 == 0, from_after, from_before)

    def chunk(c):
        field, first = c // 2, (c % 2) * 8

        def level(i, _):
            z = first + i
            k = field * 16 + z
            tile = wind[field, z]
            center = tile.astype(F32)
            above = wind[field, lax.rem(z + 1, 16)].astype(F32)
            below = wind[field, lax.rem(z + 15, 16)].astype(F32)
            around = jnp.where(z < 15, above, 0.0) + jnp.where(z > 0, below, 0.0)
            around += jnp.dot(near_x[...], tile, preferred_element_type=F32)
            around += jnp.dot(tile, near_y[...], preferred_element_type=F32)
            side = pltpu.roll(merged[...], 127 - 2 * k, 1)
            around += jnp.where((lane == 0) | (lane == 127), side, 0.0)
            around += jnp.where(line == 0, line_in[0, pl.ds(k, 1), :], 0.0)
            around += jnp.where(line == BLOCK - 1, line_in[1, pl.ds(k, 1), :], 0.0)
            stepped = center + diffusion_number * (around - 6.0 * center)
            advanced[field, z] = jnp.where(z >= terrain[...], stepped, 0.0).astype(BF16)
            return 0

        lax.fori_loop(0, 8, level, 0, unroll=2)
        return advanced.at[field, pl.ds(first, 8)]

    def send(n, dy, dz):
        c = lax.rem(y + dy, 4) * 2 + lax.rem(z_lo + dz, 2)
        part = advanced.at[c // 2, pl.ds((c % 2) * 8, 8)]
        if dz == 1 and dy > 0:
            return remote(part, relay.at[dy - 1], send_sem.at[n], relay_recv.at[dy - 1], beside)
        return remote(part, rows.at[gx], send_sem.at[n], recv_sem.at[dy * 2 + dz - 1], (c, gy, ft))

    def pass_along(dy):
        arrived = relay.at[dy - 1]
        remote(arrived, arrived, relay_send.at[dy - 1], relay_recv.at[dy - 1], beside).wait_recv()
        target = (lax.rem(y + dy, 4) * 2 + z_lo, gy, ft)
        copy = remote(arrived, rows.at[beside[0]], relay_send.at[dy - 1], recv_sem.at[dy * 2], target)
        copy.start()
        sent.append(copy)

    sent, written = [], []

    def write(src, dst, sem):
        copy = pltpu.make_async_copy(src, dst, sem)
        copy.start()
        written.append(copy)

    def write_out(n, c):
        part = (c // 2, pl.ds((c % 2) * 8, 8))
        write(advanced.at[part], advanced_out.at[part], out_sem.at[n])

    for n, (dy, dz) in enumerate(((2, 1), (1, 0), (1, 1), (3, 0), (3, 1), (2, 0), (0, 1))):
        chunk(lax.rem(y + dy, 4) * 2 + lax.rem(z_lo + dz, 2))
        copy = send(n, dy, dz)
        copy.start()
        sent.append(copy)
        write_out(n, lax.rem(y + dy, 4) * 2 + lax.rem(z_lo + dz, 2))
        if n == 1:
            own_basis.wait()
            for copy in basis_copies:
                copy.wait()
            spread_far = remote(basis_rows(piece, 16), basis_rows(piece, 16), basis_send.at[7], basis_recv.at[7], far)
            spread_far.start()
        if n == 3:
            pass_along(2)
            spread_far.wait()
            two = piece - z_hi * 16
            spread_sides = [
                remote(basis_rows(two, 32), basis_rows(two, 32), basis_send.at[8 + k], basis_recv.at[8 + k], device)
                for k, device in enumerate(sides)
            ]
            for copy in spread_sides:
                copy.start()
        if n == 5:
            pass_along(1)
    own = pltpu.make_async_copy(chunk(gx), rows.at[gx], own_sem)
    own.start()
    write_out(7, gx)
    own.wait()
    pass_along(3)

    def store(s):
        return pl.ds(pl.multiple_of(((s % 2) * 18 + s // 2) * BLOCK, BLOCK), BLOCK)

    def block(s):
        j = s % 8
        i = (j + s // 8) % 8
        left = jnp.concatenate([rows[j, z] for z in range(8)], axis=1)
        right = jnp.concatenate([rows[i, z] for z in range(8)], axis=1)
        partial[store(s), :] = lax.dot_general(left, right, (((1,), (1,)), ((), ())), preferred_element_type=F32)

        @pl.when(s % 2 != core)
        def _():
            swap(s // 2).start()

    def swap(n):
        src = partial.at[pl.ds(pl.multiple_of(((1 - core) * 18 + n) * BLOCK, BLOCK), BLOCK)]
        return remote(src, half_in.at[n], pair_send.at[n], pair_recv.at[n], sibling)

    def away(offset):
        return lax.rem(y + 4 - offset // 2, 4) * 2 + lax.rem(z_lo + offset, 2)

    arrivals = (0, 2, 6, 5, 4, 3, 7, 1)
    for n, offset in enumerate(arrivals):
        source = away(offset)
        if n > 0:
            there = rows.at[source]
            remote(there, there, send_sem.at[0], recv_sem.at[offset - 1], (source, gy, ft)).wait_recv()

        def pair(k, code):
            first = away(code % 8)
            d = (source + 8 - first) % 8
            far_side = d // 5
            half_way = d // 4 - far_side
            block(
                (1 - far_side - half_way) * (d * 8 + first)
                + far_side * ((8 - d) * 8 + source)
                + half_way * (32 + first % 4)
            )
            return code // 8

        lax.fori_loop(0, n + 1, pair, sum(o * 8**k for k, o in enumerate(arrivals)))
    write(rows, rows_out, out_sem.at[8])
    for copy in spread_sides:
        copy.wait()
    eight = core * 128
    spread_pair = remote(basis_rows(eight, 128), basis_rows(eight, 128), basis_send.at[11], basis_recv.at[11], sibling)

    mine = pl.multiple_of(core * HALF, HALF)
    other = pl.multiple_of((1 - core) * HALF, HALF)

    def take(n, _):
        swap(n).wait()
        here = pl.ds(pl.multiple_of(mine + n * BLOCK, BLOCK), BLOCK)
        partial[here, :] = partial[here, :] + half_in[n]
        return 0

    lax.fori_loop(0, 18, take, 0)
    spread_pair.start()

    def add(first, count, sources, tile):
        def body(k, _):
            here = pl.ds(pl.multiple_of(first + k * tile, 8), tile)
            there = pl.ds(pl.multiple_of(k * tile, 8), tile)
            total = partial[here, :]
            for source in sources:
                total = total + source[there, :]
            partial[here, :] = total
            return 0

        lax.fori_loop(0, count // tile, body, 0)

    starts = [[mine + p * PART] for p in range(3)]
    sizes = [PART // 4, PART // 16, PART // 64]
    for depth, (inbox, send, recv) in enumerate(((in_1, send_1, recv_1), (in_2, send_2, recv_2), (in_3, send_3, recv_3))):
        size = sizes[depth]
        copies = []
        for o in (1, 3, 2):
            for p in range(3):
                t, device = peer((p + depth) % 3, o)
                src = pl.ds(pl.multiple_of(starts[p][depth] + t * size, 8), size)
                n = p * 3 + o - 1
                copies.append(remote(partial.at[src], inbox.at[n], send.at[n], recv.at[n], device))
        for copy in copies:
            copy.start()
        for copy in copies:
            copy.wait()
        for p in range(3):
            first = starts[p][depth] + coords[(p + depth) % 3] * size
            starts[p].append(first)
            add(first, size, [inbox.at[p * 3 + o] for o in range(3)], min(size, 96))

    spread_pair.wait()
    write(basis, basis_out, out_sem.at[9])
    for p in range(3):
        here = pl.ds(pl.multiple_of(starts[p][3], 8), sizes[2])
        gram[here, :] = partial[here, :]
    lasts = []

    def pass_on(p, first, n):
        here = gram.at[pl.ds(pl.multiple_of(first, 8), sizes[0])]
        copy = remote(here, here, last_send.at[n], last_recv.at[n], sibling)
        copy.start()
        lasts.append(copy)
        write(here, gram_out.at[pl.ds(pl.multiple_of(first, 8), sizes[0])], gram_sem.at[n])

    for depth, send, recv in ((2, back_3, home_3), (1, back_2, home_2), (0, back_1, home_1)):
        size = sizes[depth]
        copies = []
        for o in (1, 3, 2):
            for p in range(3):
                here = gram.at[pl.ds(pl.multiple_of(starts[p][depth + 1], 8), size)]
                _, device = peer((p + depth) % 3, o)
                n = p * 3 + o - 1
                copies.append(remote(here, here, send.at[n], recv.at[n], device))
        for copy in copies:
            copy.start()
        if depth == 0:
            for p in range(3):
                pass_on(p, starts[p][1], p * 4)
        for o in (1, 3, 2):
            for p in range(3):
                n = p * 3 + o - 1
                t, device = peer((p + depth) % 3, 4 - o)
                first = starts[p][depth] + t * size
                there = gram.at[pl.ds(pl.multiple_of(first, 8), size)]
                remote(there, there, send.at[n], recv.at[n], device).wait_recv()
                if depth == 0:
                    pass_on(p, first, p * 4 + o)
        for copy in copies:
            copy.wait_send()
    for p in range(3):
        for o in range(4):
            n = p * 4 + o
            t = lax.rem(coords[p] + 4 - o, 4)
            where = pl.ds(pl.multiple_of(other + p * PART + t * sizes[0], 8), sizes[0])
            there = gram.at[where]
            remote(there, there, last_send.at[n], last_recv.at[n], sibling).wait_recv()
            write(there, gram_out.at[where], gram_sem.at[12 + n])
    for copy in lasts:
        copy.wait_send()
    for copy in written:
        copy.wait()

    for copy in sent:
        copy.wait_send()


def step_and_gram(wind_field, terrain, start_basis):
    dma = pltpu.SemaphoreType.DMA
    return pl.pallas_call(
        gram_kernel,
        out_shape=(
            jax.ShapeDtypeStruct((4, 16, BLOCK, 128), BF16),
            jax.ShapeDtypeStruct((GX, 8, BLOCK, 128), BF16),
            jax.ShapeDtypeStruct((PAIRS * BLOCK, BLOCK), F32),
            jax.ShapeDtypeStruct((GX, BLOCK, BLOCK), F32),
        ),
        in_specs=[pl.BlockSpec(memory_space=VMEM)] * 3,
        out_specs=(pl.BlockSpec(memory_space=pl.ANY),) * 4,
        scratch_shapes=[
            VMEM((4, 16, BLOCK, 128), BF16),
            VMEM((GX, 8, BLOCK, 128), BF16),
            VMEM((PAIRS * BLOCK, BLOCK), F32),
            VMEM((GX, BLOCK, BLOCK), F32),
            dma((10,)), dma((24,)),
            VMEM((BLOCK, 128), BF16),
            VMEM((2, BLOCK, 128), BF16),
            VMEM((2, 64, 128), F32),
            VMEM((2, 64, 128), F32),
            VMEM((BLOCK, 128), F32),
            VMEM((BLOCK, BLOCK), BF16),
            VMEM((128, 128), BF16),
            VMEM((3, 8, BLOCK, 128), BF16),
            VMEM((PAIRS * BLOCK, BLOCK), F32),
            VMEM((18, BLOCK, BLOCK), F32),
            VMEM((9, PART // 4, BLOCK), F32),
            VMEM((9, PART // 16, BLOCK), F32),
            VMEM((9, PART // 64, BLOCK), F32),
            dma((4,)), dma((4,)), dma((7,)), dma((7,)), dma((3,)), dma((3,)), dma, dma((12,)), dma((12,)), dma,
            dma((18,)), dma((18,)),
        ]
        + [dma((9,))] * 12
        + [dma((12,))] * 2,
        compiler_params=pltpu.CompilerParams(collective_id=0, has_side_effects=True, vmem_limit_bytes=LIMIT),
        name="step_and_gram",
    )(wind_field, terrain, start_basis)


def core_kernel(basis_t, rows, core, stage, outbox, inbox, send_sem, recv_sem):
    gx, gy, ft = place()
    peers = [(lax.rem(gx + i, GX), gy, ft) for i in range(1, GX)]
    all_here = greet(peers)
    for z in range(0, 8, 2):
        total = jnp.zeros((BLOCK, BLOCK), F32)
        for j in range(GX):
            pair = jnp.concatenate([rows[j, z], rows[j, z + 1]], axis=1)
            total += jnp.dot(basis_t[:, j * BLOCK : (j + 1) * BLOCK], pair, preferred_element_type=F32)
        stage[:, z, :] = total[:, :128]
        stage[:, z + 1, :] = total[:, 128:]
    for r in range(GX):
        outbox[r] = stage[r * 32 : (r + 1) * 32].reshape(BLOCK, 128).astype(BF16)
    copies = []
    for i in range(1, GX):
        device = peers[i - 1]
        copies.append(remote(outbox.at[device[0]], inbox.at[gx], send_sem.at[i - 1], recv_sem.at[i - 1], device))
    all_here()
    for copy in copies:
        copy.start()
    inbox[gx] = outbox[gx]
    for i in range(1, GX):
        there = inbox.at[lax.rem(gx + GX - i, GX)]
        remote(there, there, send_sem.at[i - 1], recv_sem.at[i - 1], peers[GX - 1 - i]).wait_recv()
    for f in range(4):
        low = inbox[2 * f].astype(F32).reshape(32, 8, 128)
        high = inbox[2 * f + 1].astype(F32).reshape(32, 8, 128)
        core[:, f] = jnp.concatenate([low, high], axis=1).astype(BF16)
    for copy in copies:
        copy.wait_send()


def core_of(basis_t, rows):
    return pl.pallas_call(
        core_kernel,
        out_shape=jax.ShapeDtypeStruct((32, 4, 16, 128), BF16),
        in_specs=[pl.BlockSpec(memory_space=VMEM)] * 2,
        out_specs=pl.BlockSpec(memory_space=VMEM),
        scratch_shapes=[
            VMEM((BLOCK, 8, 128), F32),
            VMEM((GX, BLOCK, 128), BF16),
            VMEM((GX, BLOCK, 128), BF16),
            pltpu.SemaphoreType.DMA((7,)),
            pltpu.SemaphoreType.DMA((7,)),
        ],
        compiler_params=pltpu.CompilerParams(collective_id=1, has_side_effects=True, vmem_limit_bytes=LIMIT),
        name="core",
    )(basis_t, rows)


PANEL = 64
EXACT = lax.Precision.HIGHEST


def split(value):
    high = value.astype(BF16)
    return high, (value - high.astype(F32)).astype(BF16)


def eliminate(block):
    count = PANEL // 8
    line = lax.broadcasted_iota(jnp.int32, (8, 128), 0)
    lane = lax.broadcasted_iota(jnp.int32, (8, 128), 1)
    tiles = [jnp.where(lane == line + 8 * i, 1.0, block[8 * i : 8 * i + 8]) for i in range(count)]
    for g in range(count):
        first = PANEL + 8 * g
        spread = [[jnp.broadcast_to(tiles[i][:, first + t : first + t + 1], (8, 128)) for t in range(8)] for i in range(g, count)]
        scale = jnp.zeros((8, 128), F32)
        for t in range(8):
            pivot = jnp.broadcast_to(spread[0][t][t : t + 1], (8, 128))
            inverse = 1.0 / pivot
            scale = jnp.where(line == t, lax.rsqrt(pivot), scale)
            row = jnp.broadcast_to(tiles[g][t : t + 1], (8, 128))
            heads = [jnp.broadcast_to(spread[0][u][t : t + 1], (8, 128)) for u in range(t + 1, 8)]
            for n, i in enumerate(range(g, count)):
                factor = spread[n][t] * inverse
                if n == 0:
                    factor = jnp.where(line > t, factor, 0.0)
                tiles[i] = tiles[i] - factor * row
                for u in range(t + 1, 8):
                    spread[n][u] = spread[n][u] - factor * heads[u - t - 1]
        tiles[g] = tiles[g] * scale
    return jnp.concatenate(tiles, axis=0)


def invert_factor(work, beside=lambda k: None):
    for k in range(BLOCK // PANEL):
        here = slice(k * PANEL, (k + 1) * PANEL)
        base = (k // 2) * 128
        both = work[here, base : base + 128]
        if k % 2 == 0:
            both = pltpu.roll(both, PANEL, 1)
        lane = lax.broadcasted_iota(jnp.int32, both.shape, 1)
        beside(2 * k)
        small = eliminate(jnp.where(lane < PANEL, 0.0, both))[:, :PANEL]
        beside(2 * k + 1)
        left, right = base, BLOCK + (k // 2 + 1) * 128
        rows = jnp.dot(small, work[here, left:right], precision=EXACT, preferred_element_type=F32)
        work[here, left:right] = rows
        if k + 1 < BLOCK // PANEL:
            below = (k + 1) * PANEL
            factor = rows[:, below - left : BLOCK - left]
            work[below:, left:right] = work[below:, left:right] - lax.dot_general(
                factor, rows, (((0,), (0,)), ((), ())), precision=EXACT, preferred_element_type=F32
            )


def iterate_kernel(
    blocks_in, start_in, basis, rounded, blocks, start, load_sem, high_g,
    low_g, parts, image, current, work,
):
    gx = lax.axis_index("gx")

    loads = [pltpu.make_async_copy(start_in, start, load_sem.at[0])]
    for k in range(4):
        some = pl.ds(k * 9 * BLOCK, 9 * BLOCK)
        loads.append(pltpu.make_async_copy(blocks_in.at[some], blocks.at[some], load_sem.at[k + 1]))
    for copy in loads:
        copy.start()

    def spread(n, _):
        s = (n % 18) * 2 + n // 18
        j = s % 8
        i = (j + s // 8) % 8
        block = blocks[pl.ds(pl.multiple_of(n * BLOCK, BLOCK), BLOCK), :]
        for row, column, value in ((j, i, block), (i, j, block.T)):
            high, low = split(value)
            high_g[column, pl.ds(pl.multiple_of(row * BLOCK, BLOCK), BLOCK), :] = high
            low_g[column, pl.ds(pl.multiple_of(row * BLOCK, BLOCK), BLOCK), :] = low
        return 0


    def columns(j):
        return pl.ds(pl.multiple_of(j * BLOCK, BLOCK), BLOCK)

    def keep(j, value):
        high, low = split(value)
        parts[0:BLOCK, columns(j)] = high
        parts[BLOCK:, columns(j)] = low

    def load(j, _):
        keep(j, start[j].T)
        return 0

    loads[0].wait()
    lax.fori_loop(0, GX, load, 0)
    for k in range(4):
        loads[k + 1].wait()
        lax.fori_loop(k * 9, k * 9 + 9, spread, 0, unroll=3)
    unit = jnp.where(
        lax.broadcasted_iota(jnp.int32, (BLOCK, BLOCK), 0) == lax.broadcasted_iota(jnp.int32, (BLOCK, BLOCK), 1), 1.0, 0.0
    )

    across = (((1,), (1,)), ((), ()))

    def times_gram(source, j):
        both = jnp.dot(source[...], high_g[j], preferred_element_type=F32)
        return both[:BLOCK] + (both[BLOCK:] + jnp.dot(source[0:BLOCK, :], low_g[j], preferred_element_type=F32))

    def clear():
        work[...] = jnp.zeros((BLOCK, 2 * BLOCK), F32)

    def add_products(j, value):
        high, middle = split(value)
        low = (value - high.astype(F32) - middle.astype(F32)).astype(BF16)
        image[0:BLOCK, columns(j)] = high
        image[BLOCK:, columns(j)] = middle
        three = lax.dot_general(jnp.concatenate([high, middle, low], axis=0), high, across, preferred_element_type=F32)
        work[:, 0:BLOCK] += three[:BLOCK] + lax.dot_general(middle, middle, across, preferred_element_type=F32)
        work[:, BLOCK:] += three[BLOCK : 2 * BLOCK] + three[2 * BLOCK :]

    def inverse_factor(beside):
        mixed = work[:, BLOCK:]
        work[:, 0:BLOCK] += mixed + mixed.T
        work[:, BLOCK:] = unit
        invert_factor(work, beside)
        high, low = split(work[:, BLOCK:])
        return jnp.concatenate([high, low], axis=0)

    def times_factor(factor, source, j):
        both = jnp.dot(factor, source[0:BLOCK, columns(j)], preferred_element_type=F32)
        return both[:BLOCK] + (
            both[BLOCK:] + jnp.dot(factor[:BLOCK], source[BLOCK:, columns(j)], preferred_element_type=F32)
        )

    def first(j, _):
        add_products(j, times_gram(parts, j))
        return 0

    clear()
    lax.fori_loop(0, GX, first, 0, unroll=2)

    def beside(j):
        keep(j, times_gram(image, j))

    def iteration(_, carry):
        factor = inverse_factor(beside)
        clear()

        def apply(j, _):
            add_products(j, times_factor(factor, parts, j))
            return 0

        lax.fori_loop(0, GX, apply, 0, unroll=4)
        return carry

    lax.fori_loop(0, ITERS - 1, iteration, 0)
    factor = inverse_factor(lambda j: None)

    def last(j, _):
        value = times_factor(factor, image, j)
        current[:, columns(j)] = value
        parts[0:BLOCK, columns(j)] = value.astype(BF16)
        return 0

    lax.fori_loop(0, GX, last, 0, unroll=4)
    basis[...] = current[:, columns(gx)].T
    rounded[...] = parts[0:BLOCK, :]


def iterate(blocks, start):
    return pl.pallas_call(
        iterate_kernel,
        out_shape=(jax.ShapeDtypeStruct((BLOCK, BLOCK), F32), jax.ShapeDtypeStruct((BLOCK, GX * BLOCK), BF16)),
        in_specs=[pl.BlockSpec(memory_space=pl.ANY)] * 2,
        out_specs=(pl.BlockSpec(memory_space=VMEM),) * 2,
        scratch_shapes=[
            VMEM((PAIRS * BLOCK, BLOCK), F32),
            VMEM((GX, BLOCK, BLOCK), F32),
            pltpu.SemaphoreType.DMA((5,)),
            VMEM((GX, GX * BLOCK, BLOCK), BF16),
            VMEM((GX, GX * BLOCK, BLOCK), BF16),
            VMEM((2 * BLOCK, GX * BLOCK), BF16),
            VMEM((2 * BLOCK, GX * BLOCK), BF16),
            VMEM((BLOCK, GX * BLOCK), F32),
            VMEM((BLOCK, 2 * BLOCK), F32),
        ],
        compiler_params=pltpu.CompilerParams(vmem_limit_bytes=LIMIT),
        name="iterate",
    )(blocks, start)


def per_device(wind_field, terrain, start_basis):
    advanced, rows, blocks, basis = step_and_gram(wind_field, terrain, start_basis)
    basis_rows, rounded = iterate(blocks, basis)
    core = core_of(rounded, rows)
    return (advanced, basis_rows, core)


def solution(mesh):
    placed = (P("ft", None, "gx", "gy"), P("gx", "gy"), P("gx", None))
    return jax.shard_map(
        per_device,
        mesh=mesh,
        in_specs=placed,
        out_specs=(P("ft", None, "gx", "gy"), P("gx", None), P("gx", "ft", None, "gy")),
        check_vma=False,
    )
```

```python
import functools

import jax
import jax.numpy as jnp
from jax import lax
from jax.experimental import pallas as pl
from jax.experimental.pallas import tpu as pltpu
from jax.sharding import PartitionSpec as P

ITERS = 4
MESH = pl.DeviceIdType.MESH
VMEM = pltpu.VMEM
F32 = jnp.float32
BF16 = jnp.bfloat16
GX = 8
BLOCK = 256
PAIRS = 36
LIMIT = 56 * 1024 * 1024

diffusion_number = 0.15


def place():
    return lax.axis_index("gx"), lax.axis_index("gy"), lax.axis_index("ft")


def greet(devices):
    barrier = pltpu.get_barrier_semaphore()
    for device in devices:
        pl.semaphore_signal(barrier, inc=1, device_id=device, device_id_type=MESH)
    return lambda: pl.semaphore_wait(barrier, len(devices))


def remote(src, dst, send, recv, device):
    return pltpu.make_async_remote_copy(
        src_ref=src, dst_ref=dst, send_sem=send, recv_sem=recv, device_id=device, device_id_type=MESH
    )


HALF = 18 * BLOCK
PART = HALF // 3


def gram_kernel(
    wind, terrain, start, advanced_out, rows_out, gram_out, basis_out,
    advanced, rows, gram, basis, out_sem, gram_sem,
    edge_out, edge_in, line_out, line_in, merged, near_x, near_y,
    relay, partial, half_in, long_1, long_2, long_3, short_1, short_2, short_3,
    halo_send, halo_recv, send_sem, recv_sem, relay_send, relay_recv, own_sem, basis_send, basis_recv, basis_own,
    pair_send, pair_recv, sum_send, sum_recv, back_send, back_recv, last_send, last_recv,
):
    gx, gy, ft = place()
    core, z_hi = ft % 2, ft // 2
    coords = (gy, gx // 2, z_hi * 2 + gx % 2)

    def at(axis, t):
        if axis == 0:
            return (gx, t, ft)
        if axis == 1:
            return (t * 2 + gx % 2, gy, ft)
        return ((gx // 2) * 2 + t % 2, gy, (t // 2) * 2 + core)

    def peer(axis, o):
        t = lax.rem(coords[axis] + o, 4)
        return t, at(axis, t)

    y, z_lo = gx // 2, gx % 2
    beside = (y * 2 + 1 - z_lo, gy, ft)
    peers = [(lax.rem(gx + i, GX), gy, ft) for i in range(1, GX)]
    sides = [(gx, lax.rem(gy + o, 4), ft) for o in range(1, 4)]
    sibling = (gx, gy, z_hi * 2 + 1 - core)
    far = (gx, gy, lax.rem(ft + 2, 4))
    far_odd = ((gx // 2) * 2 + 1 - gx % 2, gy, lax.rem(ft + 2, 4))
    all_here = greet(peers + sides + [sibling, far, far_odd])

    def basis_rows(first, count):
        return basis.at[:, pl.ds(pl.multiple_of(first, 16), count)]

    piece = (core * 8 + gy * 2 + z_hi) * 16
    here = pl.ds(pl.multiple_of(piece, 16), 16)
    lane = lax.broadcasted_iota(jnp.int32, (BLOCK, 128), 1)
    line = lax.broadcasted_iota(jnp.int32, (BLOCK, 128), 0)

    def collect(k, packed):
        tile = wind[k // 16, k % 16].astype(F32)
        line_out[0, pl.ds(k, 1), :] = tile[0:1]
        line_out[1, pl.ds(k, 1), :] = tile[BLOCK - 1 : BLOCK]
        return jnp.where(lane // 2 == k, pltpu.roll(tile, 2 * k + 1, 1), packed)

    packed = lax.fori_loop(0, 64, collect, jnp.zeros((BLOCK, 128), F32), unroll=2)
    edge_out[...] = packed.astype(BF16)
    halos = [
        remote(line_out.at[1], line_in.at[0], halo_send.at[0], halo_recv.at[0], peers[0]),
        remote(line_out.at[0], line_in.at[1], halo_send.at[1], halo_recv.at[1], peers[6]),
        remote(edge_out, edge_in.at[0], halo_send.at[2], halo_recv.at[2], sides[0]),
        remote(edge_out, edge_in.at[1], halo_send.at[3], halo_recv.at[3], sides[2]),
    ]
    all_here()
    for copy in halos:
        copy.start()
    basis_copies = [
        remote(start.at[here], basis.at[gx, here], basis_send.at[n], basis_recv.at[n], device) for n, device in enumerate(peers)
    ]
    for copy in basis_copies:
        copy.start()
    own_basis = pltpu.make_async_copy(start.at[here], basis.at[gx, here], basis_own)
    own_basis.start()
    a = lax.broadcasted_iota(jnp.int32, (BLOCK, BLOCK), 0)
    b = lax.broadcasted_iota(jnp.int32, (BLOCK, BLOCK), 1)
    near_x[...] = jnp.where(jnp.abs(a - b) == 1, 1.0, 0.0).astype(BF16)
    near_y[...] = near_x[0:128, 0:128]
    for copy in halos:
        copy.wait()
    from_before = pltpu.roll(edge_in[0].astype(F32), 1, 1)
    from_after = pltpu.roll(edge_in[1].astype(F32), 127, 1)
    merged[...] = jnp.where(lane % 2 == 0, from_after, from_before)

    def chunk(c):
        field, first = c // 2, (c % 2) * 8

        def level(i, _):
            z = first + i
            k = field * 16 + z
            tile = wind[field, z]
            center = tile.astype(F32)
            above = wind[field, lax.rem(z + 1, 16)].astype(F32)
            below = wind[field, lax.rem(z + 15, 16)].astype(F32)
            around = jnp.where(z < 15, above, 0.0) + jnp.where(z > 0, below, 0.0)
            around += jnp.dot(near_x[...], tile, preferred_element_type=F32)
            around += jnp.dot(tile, near_y[...], preferred_element_type=F32)
            side = pltpu.roll(merged[...], 127 - 2 * k, 1)
            around += jnp.where((lane == 0) | (lane == 127), side, 0.0)
            around += jnp.where(line == 0, line_in[0, pl.ds(k, 1), :], 0.0)
            around += jnp.where(line == BLOCK - 1, line_in[1, pl.ds(k, 1), :], 0.0)
            stepped = center + diffusion_number * (around - 6.0 * center)
            advanced[field, z] = jnp.where(z >= terrain[...], stepped, 0.0).astype(BF16)
            return 0

        lax.fori_loop(0, 8, level, 0, unroll=2)
        return advanced.at[field, pl.ds(first, 8)]

    def send(n, dy, dz):
        c = lax.rem(y + dy, 4) * 2 + lax.rem(z_lo + dz, 2)
        part = advanced.at[c // 2, pl.ds((c % 2) * 8, 8)]
        if dz == 1 and dy > 0:
            return remote(part, relay.at[dy - 1], send_sem.at[n], relay_recv.at[dy - 1], beside)
        return remote(part, rows.at[gx], send_sem.at[n], recv_sem.at[dy * 2 + dz - 1], (c, gy, ft))

    def pass_along(dy):
        arrived = relay.at[dy - 1]
        remote(arrived, arrived, relay_send.at[dy - 1], relay_recv.at[dy - 1], beside).wait_recv()
        target = (lax.rem(y + dy, 4) * 2 + z_lo, gy, ft)
        copy = remote(arrived, rows.at[beside[0]], relay_send.at[dy - 1], recv_sem.at[dy * 2], target)
        copy.start()
        sent.append(copy)

    sent, written = [], []

    def write(src, dst, sem):
        copy = pltpu.make_async_copy(src, dst, sem)
        copy.start()
        written.append(copy)

    def write_out(n, c):
        part = (c // 2, pl.ds((c % 2) * 8, 8))
        write(advanced.at[part], advanced_out.at[part], out_sem.at[n])

    for n, (dy, dz) in enumerate(((2, 1), (1, 0), (1, 1), (3, 0), (3, 1), (2, 0), (0, 1))):
        chunk(lax.rem(y + dy, 4) * 2 + lax.rem(z_lo + dz, 2))
        copy = send(n, dy, dz)
        copy.start()
        sent.append(copy)
        write_out(n, lax.rem(y + dy, 4) * 2 + lax.rem(z_lo + dz, 2))
        if n == 1:
            own_basis.wait()
            for copy in basis_copies:
                copy.wait()
            spread_far = remote(basis_rows(piece, 16), basis_rows(piece, 16), basis_send.at[7], basis_recv.at[7], far)
            spread_far.start()
        if n == 3:
            pass_along(2)
            spread_far.wait()
            two = piece - z_hi * 16
            spread_sides = [
                remote(basis_rows(two, 32), basis_rows(two, 32), basis_send.at[8 + k], basis_recv.at[8 + k], device)
                for k, device in enumerate(sides)
            ]
            for copy in spread_sides:
                copy.start()
        if n == 5:
            pass_along(1)
    own = pltpu.make_async_copy(chunk(gx), rows.at[gx], own_sem)
    own.start()
    write_out(7, gx)
    own.wait()
    pass_along(3)

    def store(s):
        return pl.ds(pl.multiple_of(((s % 2) * 18 + s // 2) * BLOCK, BLOCK), BLOCK)

    def block(s):
        j = s % 8
        i = (j + s // 8) % 8
        left = jnp.concatenate([rows[j, z] for z in range(8)], axis=1)
        right = jnp.concatenate([rows[i, z] for z in range(8)], axis=1)
        partial[store(s), :] = lax.dot_general(left, right, (((1,), (1,)), ((), ())), preferred_element_type=F32)

        @pl.when(s % 2 != core)
        def _():
            swap(s // 2).start()

    def swap(n):
        src = partial.at[pl.ds(pl.multiple_of(((1 - core) * 18 + n) * BLOCK, BLOCK), BLOCK)]
        return remote(src, half_in.at[n], pair_send.at[n], pair_recv.at[n], sibling)

    def away(offset):
        return lax.rem(y + 4 - offset // 2, 4) * 2 + lax.rem(z_lo + offset, 2)

    arrivals = (0, 2, 6, 5, 4, 3, 7, 1)
    for n, offset in enumerate(arrivals):
        source = away(offset)
        if n > 0:
            there = rows.at[source]
            remote(there, there, send_sem.at[0], recv_sem.at[offset - 1], (source, gy, ft)).wait_recv()

        def pair(k, code):
            first = away(code % 8)
            d = (source + 8 - first) % 8
            far_side = d // 5
            half_way = d // 4 - far_side
            block(
                (1 - far_side - half_way) * (d * 8 + first)
                + far_side * ((8 - d) * 8 + source)
                + half_way * (32 + first % 4)
            )
            return code // 8

        lax.fori_loop(0, n + 1, pair, sum(o * 8**k for k, o in enumerate(arrivals)))
    write(rows, rows_out, out_sem.at[8])
    for copy in spread_sides:
        copy.wait()
    eight = core * 128
    spread_pair = remote(basis_rows(eight, 128), basis_rows(eight, 128), basis_send.at[11], basis_recv.at[11], sibling)

    mine = pl.multiple_of(core * HALF, HALF)
    other = pl.multiple_of((1 - core) * HALF, HALF)

    def take(n, _):
        swap(n).wait()
        here = pl.ds(pl.multiple_of(mine + n * BLOCK, BLOCK), BLOCK)
        partial[here, :] = partial[here, :] + half_in[n]
        return 0

    lax.fori_loop(0, 18, take, 0)
    spread_pair.start()

    def add(first, count, sources, tile):
        def body(k, _):
            here = pl.ds(pl.multiple_of(first + k * tile, 8), tile)
            there = pl.ds(pl.multiple_of(k * tile, 8), tile)
            total = partial[here, :]
            for source in sources:
                total = total + source[there, :]
            partial[here, :] = total
            return 0

        lax.fori_loop(0, count // tile, body, 0)

    runs = ((0, 1024), (1024, 512))
    sizes = [[count // 4, count // 16, count // 64] for _, count in runs]
    boxes = ((long_1, long_2, long_3), (short_1, short_2, short_3))
    starts = [[[mine + p * PART + offset] for p in range(3)] for offset, _ in runs]
    lasts = []

    def span(first, size):
        return pl.ds(pl.multiple_of(first, 8), size)

    def reduce_start(q, depth):
        size, copies = sizes[q][depth], []
        for o in (1, 3, 2):
            for p in range(3):
                t, device = peer((p + depth) % 3, o)
                n = p * 3 + o - 1
                src = partial.at[span(starts[q][p][depth] + t * size, size)]
                copies.append(remote(src, boxes[q][depth].at[n], sum_send.at[q, depth, n], sum_recv.at[q, depth, n], device))
        for copy in copies:
            copy.start()
        return copies

    def reduce_finish(q, depth, copies):
        size = sizes[q][depth]
        for copy in copies:
            copy.wait()
        for p in range(3):
            first = starts[q][p][depth] + coords[(p + depth) % 3] * size
            starts[q][p].append(first)
            add(first, size, [boxes[q][depth].at[p * 3 + o] for o in range(3)], min(size, 64))

    def pass_on(q, p, o, first):
        n = (q * 3 + p) * 4 + o
        here = span(first, sizes[q][0])
        copy = remote(gram.at[here], gram.at[here], last_send.at[n], last_recv.at[n], sibling)
        copy.start()
        lasts.append(copy)
        write(gram.at[here], gram_out.at[here], gram_sem.at[n])

    def gather_start(q, depth):
        size, copies = sizes[q][depth], []
        if depth == 2:
            for p in range(3):
                here = span(starts[q][p][3], size)
                gram[here, :] = partial[here, :]
        for o in (1, 3, 2):
            for p in range(3):
                here = gram.at[span(starts[q][p][depth + 1], size)]
                _, device = peer((p + depth) % 3, o)
                n = p * 3 + o - 1
                copies.append(remote(here, here, back_send.at[q, depth, n], back_recv.at[q, depth, n], device))
        for copy in copies:
            copy.start()
        lasts.extend(copies)
        if depth == 0:
            for p in range(3):
                pass_on(q, p, 0, starts[q][p][1])

    def gather_finish(q, depth):
        size = sizes[q][depth]
        for o in (1, 3, 2):
            for p in range(3):
                n = p * 3 + o - 1
                t, device = peer((p + depth) % 3, 4 - o)
                first = starts[q][p][depth] + t * size
                there = gram.at[span(first, size)]
                remote(there, there, back_send.at[q, depth, n], back_recv.at[q, depth, n], device).wait_recv()
                if depth == 0:
                    pass_on(q, p, o, first)

    in_flight = [reduce_start(0, 0), reduce_start(1, 0)]
    for depth in range(3):
        for q in range(2):
            reduce_finish(q, depth, in_flight[q])
            if depth < 2:
                in_flight[q] = reduce_start(q, depth + 1)
            else:
                gather_start(q, 2)
    spread_pair.wait()
    write(basis, basis_out, out_sem.at[9])
    for depth in (2, 1, 0):
        for q in range(2):
            gather_finish(q, depth)
            if depth > 0:
                gather_start(q, depth - 1)
    for q, (offset, _) in enumerate(runs):
        for o in (0, 1, 3, 2):
            for p in range(3):
                n = (q * 3 + p) * 4 + o
                t = lax.rem(coords[p] + 4 - o, 4)
                where = span(other + p * PART + offset + t * sizes[q][0], sizes[q][0])
                there = gram.at[where]
                remote(there, there, last_send.at[n], last_recv.at[n], sibling).wait_recv()
                write(there, gram_out.at[where], gram_sem.at[24 + n])
    for copy in lasts:
        copy.wait_send()
    for copy in written:
        copy.wait()

    for copy in sent:
        copy.wait_send()


def step_and_gram(wind_field, terrain, start_basis):
    dma = pltpu.SemaphoreType.DMA
    return pl.pallas_call(
        gram_kernel,
        out_shape=(
            jax.ShapeDtypeStruct((4, 16, BLOCK, 128), BF16),
            jax.ShapeDtypeStruct((GX, 8, BLOCK, 128), BF16),
            jax.ShapeDtypeStruct((PAIRS * BLOCK, BLOCK), F32),
            jax.ShapeDtypeStruct((GX, BLOCK, BLOCK), F32),
        ),
        in_specs=[pl.BlockSpec(memory_space=VMEM)] * 3,
        out_specs=(pl.BlockSpec(memory_space=pl.ANY),) * 4,
        scratch_shapes=[
            VMEM((4, 16, BLOCK, 128), BF16),
            VMEM((GX, 8, BLOCK, 128), BF16),
            VMEM((PAIRS * BLOCK, BLOCK), F32),
            VMEM((GX, BLOCK, BLOCK), F32),
            dma((10,)), dma((48,)),
            VMEM((BLOCK, 128), BF16),
            VMEM((2, BLOCK, 128), BF16),
            VMEM((2, 64, 128), F32),
            VMEM((2, 64, 128), F32),
            VMEM((BLOCK, 128), F32),
            VMEM((BLOCK, BLOCK), BF16),
            VMEM((128, 128), BF16),
            VMEM((3, 8, BLOCK, 128), BF16),
            VMEM((PAIRS * BLOCK, BLOCK), F32),
            VMEM((18, BLOCK, BLOCK), F32),
            VMEM((9, 256, BLOCK), F32),
            VMEM((9, 64, BLOCK), F32),
            VMEM((9, 16, BLOCK), F32),
            VMEM((9, 128, BLOCK), F32),
            VMEM((9, 32, BLOCK), F32),
            VMEM((9, 8, BLOCK), F32),
            dma((4,)), dma((4,)), dma((7,)), dma((7,)), dma((3,)), dma((3,)), dma, dma((12,)), dma((12,)), dma,
            dma((18,)), dma((18,)),
        ]
        + [dma((2, 3, 9))] * 4
        + [dma((24,))] * 2,
        compiler_params=pltpu.CompilerParams(collective_id=0, has_side_effects=True, vmem_limit_bytes=LIMIT),
        name="step_and_gram",
    )(wind_field, terrain, start_basis)


def core_kernel(basis_t, rows, core, stage, outbox, inbox, send_sem, recv_sem):
    gx, gy, ft = place()
    peers = [(lax.rem(gx + i, GX), gy, ft) for i in range(1, GX)]
    all_here = greet(peers)
    for z in range(0, 8, 2):
        total = jnp.zeros((BLOCK, BLOCK), F32)
        for j in range(GX):
            pair = jnp.concatenate([rows[j, z], rows[j, z + 1]], axis=1)
            total += jnp.dot(basis_t[:, j * BLOCK : (j + 1) * BLOCK], pair, preferred_element_type=F32)
        stage[:, z, :] = total[:, :128]
        stage[:, z + 1, :] = total[:, 128:]
    for r in range(GX):
        outbox[r] = stage[r * 32 : (r + 1) * 32].reshape(BLOCK, 128).astype(BF16)
    copies = []
    for i in range(1, GX):
        device = peers[i - 1]
        copies.append(remote(outbox.at[device[0]], inbox.at[gx], send_sem.at[i - 1], recv_sem.at[i - 1], device))
    all_here()
    for copy in copies:
        copy.start()
    inbox[gx] = outbox[gx]
    for i in range(1, GX):
        there = inbox.at[lax.rem(gx + GX - i, GX)]
        remote(there, there, send_sem.at[i - 1], recv_sem.at[i - 1], peers[GX - 1 - i]).wait_recv()
    for f in range(4):
        low = inbox[2 * f].astype(F32).reshape(32, 8, 128)
        high = inbox[2 * f + 1].astype(F32).reshape(32, 8, 128)
        core[:, f] = jnp.concatenate([low, high], axis=1).astype(BF16)
    for copy in copies:
        copy.wait_send()


def core_of(basis_t, rows):
    return pl.pallas_call(
        core_kernel,
        out_shape=jax.ShapeDtypeStruct((32, 4, 16, 128), BF16),
        in_specs=[pl.BlockSpec(memory_space=VMEM)] * 2,
        out_specs=pl.BlockSpec(memory_space=VMEM),
        scratch_shapes=[
            VMEM((BLOCK, 8, 128), F32),
            VMEM((GX, BLOCK, 128), BF16),
            VMEM((GX, BLOCK, 128), BF16),
            pltpu.SemaphoreType.DMA((7,)),
            pltpu.SemaphoreType.DMA((7,)),
        ],
        compiler_params=pltpu.CompilerParams(collective_id=1, has_side_effects=True, vmem_limit_bytes=LIMIT),
        name="core",
    )(basis_t, rows)


PANEL = 64
EXACT = lax.Precision.HIGHEST


def split(value):
    high = value.astype(BF16)
    return high, (value - high.astype(F32)).astype(BF16)


def eliminate(block):
    count = PANEL // 8
    line = lax.broadcasted_iota(jnp.int32, (8, 128), 0)
    lane = lax.broadcasted_iota(jnp.int32, (8, 128), 1)
    tiles = [jnp.where(lane == line + 8 * i, 1.0, block[8 * i : 8 * i + 8]) for i in range(count)]
    for g in range(count):
        first = PANEL + 8 * g
        spread = [[jnp.broadcast_to(tiles[i][:, first + t : first + t + 1], (8, 128)) for t in range(8)] for i in range(g, count)]
        scale = jnp.zeros((8, 128), F32)
        for t in range(8):
            pivot = jnp.broadcast_to(spread[0][t][t : t + 1], (8, 128))
            inverse = 1.0 / pivot
            scale = jnp.where(line == t, lax.rsqrt(pivot), scale)
            row = jnp.broadcast_to(tiles[g][t : t + 1], (8, 128))
            heads = [jnp.broadcast_to(spread[0][u][t : t + 1], (8, 128)) for u in range(t + 1, 8)]
            for n, i in enumerate(range(g, count)):
                factor = spread[n][t] * inverse
                if n == 0:
                    factor = jnp.where(line > t, factor, 0.0)
                tiles[i] = tiles[i] - factor * row
                for u in range(t + 1, 8):
                    spread[n][u] = spread[n][u] - factor * heads[u - t - 1]
        tiles[g] = tiles[g] * scale
    return jnp.concatenate(tiles, axis=0)


def invert_factor(work, beside=lambda k: None):
    for k in range(BLOCK // PANEL):
        here = slice(k * PANEL, (k + 1) * PANEL)
        base = (k // 2) * 128
        both = work[here, base : base + 128]
        if k % 2 == 0:
            both = pltpu.roll(both, PANEL, 1)
        lane = lax.broadcasted_iota(jnp.int32, both.shape, 1)
        beside(2 * k)
        small = eliminate(jnp.where(lane < PANEL, 0.0, both))[:, :PANEL]
        beside(2 * k + 1)
        left, right = base, BLOCK + (k // 2 + 1) * 128
        rows = jnp.dot(small, work[here, left:right], precision=EXACT, preferred_element_type=F32)
        work[here, left:right] = rows
        if k + 1 < BLOCK // PANEL:
            below = (k + 1) * PANEL
            factor = rows[:, below - left : BLOCK - left]
            work[below:, left:right] = work[below:, left:right] - lax.dot_general(
                factor, rows, (((0,), (0,)), ((), ())), precision=EXACT, preferred_element_type=F32
            )


def iterate_kernel(
    blocks_in, start_in, basis, rounded, blocks, start, load_sem, high_g,
    low_g, parts, image, current, work,
):
    gx = lax.axis_index("gx")

    loads = [pltpu.make_async_copy(start_in, start, load_sem.at[0])]
    for k in range(4):
        some = pl.ds(k * 9 * BLOCK, 9 * BLOCK)
        loads.append(pltpu.make_async_copy(blocks_in.at[some], blocks.at[some], load_sem.at[k + 1]))
    for copy in loads:
        copy.start()

    def spread(n, _):
        s = (n % 18) * 2 + n // 18
        j = s % 8
        i = (j + s // 8) % 8
        block = blocks[pl.ds(pl.multiple_of(n * BLOCK, BLOCK), BLOCK), :]
        for row, column, value in ((j, i, block), (i, j, block.T)):
            high, low = split(value)
            high_g[column, pl.ds(pl.multiple_of(row * BLOCK, BLOCK), BLOCK), :] = high
            low_g[column, pl.ds(pl.multiple_of(row * BLOCK, BLOCK), BLOCK), :] = low
        return 0


    def columns(j):
        return pl.ds(pl.multiple_of(j * BLOCK, BLOCK), BLOCK)

    def keep(j, value):
        high, low = split(value)
        parts[0:BLOCK, columns(j)] = high
        parts[BLOCK:, columns(j)] = low

    def load(j, _):
        keep(j, start[j].T)
        return 0

    loads[0].wait()
    lax.fori_loop(0, GX, load, 0)
    for k in range(4):
        loads[k + 1].wait()
        lax.fori_loop(k * 9, k * 9 + 9, spread, 0, unroll=3)
    unit = jnp.where(
        lax.broadcasted_iota(jnp.int32, (BLOCK, BLOCK), 0) == lax.broadcasted_iota(jnp.int32, (BLOCK, BLOCK), 1), 1.0, 0.0
    )

    across = (((1,), (1,)), ((), ()))

    def times_gram(source, j):
        both = jnp.dot(source[...], high_g[j], preferred_element_type=F32)
        return both[:BLOCK] + (both[BLOCK:] + jnp.dot(source[0:BLOCK, :], low_g[j], preferred_element_type=F32))

    def clear():
        work[...] = jnp.zeros((BLOCK, 2 * BLOCK), F32)

    def add_products(j, value):
        high, middle = split(value)
        low = (value - high.astype(F32) - middle.astype(F32)).astype(BF16)
        image[0:BLOCK, columns(j)] = high
        image[BLOCK:, columns(j)] = middle
        three = lax.dot_general(jnp.concatenate([high, middle, low], axis=0), high, across, preferred_element_type=F32)
        work[:, 0:BLOCK] += three[:BLOCK] + lax.dot_general(middle, middle, across, preferred_element_type=F32)
        work[:, BLOCK:] += three[BLOCK : 2 * BLOCK] + three[2 * BLOCK :]

    def inverse_factor(beside):
        mixed = work[:, BLOCK:]
        work[:, 0:BLOCK] += mixed + mixed.T
        work[:, BLOCK:] = unit
        invert_factor(work, beside)
        high, low = split(work[:, BLOCK:])
        return jnp.concatenate([high, low], axis=0)

    def times_factor(factor, source, j):
        both = jnp.dot(factor, source[0:BLOCK, columns(j)], preferred_element_type=F32)
        return both[:BLOCK] + (
            both[BLOCK:] + jnp.dot(factor[:BLOCK], source[BLOCK:, columns(j)], preferred_element_type=F32)
        )

    def first(j, _):
        add_products(j, times_gram(parts, j))
        return 0

    clear()
    lax.fori_loop(0, GX, first, 0, unroll=2)

    def beside(j):
        keep(j, times_gram(image, j))

    def iteration(_, carry):
        factor = inverse_factor(beside)
        clear()

        def apply(j, _):
            add_products(j, times_factor(factor, parts, j))
            return 0

        lax.fori_loop(0, GX, apply, 0, unroll=4)
        return carry

    lax.fori_loop(0, ITERS - 1, iteration, 0)
    factor = inverse_factor(lambda j: None)

    def last(j, _):
        value = times_factor(factor, image, j)
        current[:, columns(j)] = value
        parts[0:BLOCK, columns(j)] = value.astype(BF16)
        return 0

    lax.fori_loop(0, GX, last, 0, unroll=4)
    basis[...] = current[:, columns(gx)].T
    rounded[...] = parts[0:BLOCK, :]


def iterate(blocks, start):
    return pl.pallas_call(
        iterate_kernel,
        out_shape=(jax.ShapeDtypeStruct((BLOCK, BLOCK), F32), jax.ShapeDtypeStruct((BLOCK, GX * BLOCK), BF16)),
        in_specs=[pl.BlockSpec(memory_space=pl.ANY)] * 2,
        out_specs=(pl.BlockSpec(memory_space=VMEM),) * 2,
        scratch_shapes=[
            VMEM((PAIRS * BLOCK, BLOCK), F32),
            VMEM((GX, BLOCK, BLOCK), F32),
            pltpu.SemaphoreType.DMA((5,)),
            VMEM((GX, GX * BLOCK, BLOCK), BF16),
            VMEM((GX, GX * BLOCK, BLOCK), BF16),
            VMEM((2 * BLOCK, GX * BLOCK), BF16),
            VMEM((2 * BLOCK, GX * BLOCK), BF16),
            VMEM((BLOCK, GX * BLOCK), F32),
            VMEM((BLOCK, 2 * BLOCK), F32),
        ],
        compiler_params=pltpu.CompilerParams(vmem_limit_bytes=LIMIT),
        name="iterate",
    )(blocks, start)


def per_device(wind_field, terrain, start_basis):
    advanced, rows, blocks, basis = step_and_gram(wind_field, terrain, start_basis)
    basis_rows, rounded = iterate(blocks, basis)
    core = core_of(rounded, rows)
    return (advanced, basis_rows, core)


def solution(mesh):
    placed = (P("ft", None, "gx", "gy"), P("gx", "gy"), P("gx", None))
    return jax.shard_map(
        per_device,
        mesh=mesh,
        in_specs=placed,
        out_specs=(P("ft", None, "gx", "gy"), P("gx", None), P("gx", "ft", None, "gy")),
        check_vma=False,
    )
```
